32 devices in a mesh: strip: 2 (over x), az: 4 (over z), tile: 4 (over y, core).
Axes of the slice: x: 2, y: 2, z: 4, core: 2. Of those that a mesh axis runs over, the one named last changes fastest.
Arguments:
- raw_echo: float32 [2, 4096, 4096], P(None, ('strip', 'az', 'tile')), parts along dimension 1, may hold values from -6 to 6
- phase_scaling: float32 [1024, 4096], P(None, 'tile'), may hold values from -3.140625 to 3.140625
- phase_range: float32 [1024, 4096], P('tile'), may hold values from -3.140625 to 3.140625
- phase_azimuth: float32 [1024, 4096], P(None, 'tile'), may hold values from -3.140625 to 3.140625
Outputs:
- image: float32 [2, 4096, 4096], P(None, ('strip', 'az'), 'tile'), parts along dimension 1
The draws below stay inside these ranges and needn't reach their ends.
There are 2 independent parts, one for each index of `strip`. The reference program is written for one: setup_inputs(seed, part) draws one part's arguments, and reference() takes and returns one part's arrays. A program takes and returns all parts, laid end to end along the dimension named above; an argument that names none is the same for every part. Nothing has to cross between parts.
All inputs are finite; a program needn't handle non-finite values.
Results may differ from the reference program's by a relative error of at most 0.00007.
Values sent between devices are 32-bit elements; how exact they have to be, the bound alone decides.
No kernel may reach another device: no remote copies, remote signals or barrier semaphores. Data moves between devices by JAX's collectives and lax.ppermute only.
A program may use at most 128 MiB of HBM per device.

```python
import jax
import jax.numpy as jnp
from jax import lax

RANGES = 4096
PULSES = 512
TAIL = 512
LENGTH = 1024
STRIP_PULSES = 2048
N_AZ = 4


def block_levels(stream_key, extent, cuts, low, top_value):
    def one(dim, blocks):
        steps = jax.random.uniform(jax.random.fold_in(jax.random.fold_in(stream_key, 6), dim), (blocks,), jnp.float32, low / len(cuts), top_value / len(cuts))
        return jnp.repeat(jnp.exp(steps), extent[dim] // blocks).reshape((-1,) + (1,) * (len(extent) - dim - 1))

    loudness = one(*cuts[0])
    for cut in cuts[1:]:
        loudness = loudness * one(*cut)
    return loudness


def gaussian(own_key, shape, scale, bound, shards=(), dtype=jnp.bfloat16):
    result = jax.random.normal(own_key, shape, jnp.float32) * scale
    if len(shards) > 0:
        result = block_levels(own_key, shape, shards, -0.22, 0.18) * result
    return jnp.clip(result, min=-bound, max=bound).astype(dtype)


def setup_inputs(seed: int = 0, part: int = 0) -> dict:
    key_list = jax.random.split(jax.random.key(seed), 5)
    own_keys = jax.random.split(jax.random.fold_in(key_list[4], part), 5)
    return {
        "raw_echo": gaussian(own_keys[0], (2, STRIP_PULSES, RANGES), 1.0, 6.0, ((1, 16),), jnp.float32),
        "phase_scaling": jnp.clip(jax.random.uniform(key_list[1], (LENGTH, RANGES), jnp.float32, -3.140625, 3.140625), -3.140625, 3.140625),
        "phase_range": jnp.clip(jax.random.uniform(key_list[2], (LENGTH, RANGES), jnp.float32, -3.140625, 3.140625), -3.140625, 3.140625),
        "phase_azimuth": jnp.clip(jax.random.uniform(key_list[3], (LENGTH, RANGES), jnp.float32, -3.140625, 3.140625), -3.140625, 3.140625),
    }


def reference(raw_echo, phase_scaling, phase_range, phase_azimuth):
    blocks = raw_echo.reshape(2, N_AZ, PULSES, RANGES).transpose(1, 0, 2, 3)
    turn_one = lax.complex(jnp.cos(phase_scaling), jnp.sin(phase_scaling))
    turn_two = lax.complex(jnp.cos(phase_range), jnp.sin(phase_range))
    turn_three = lax.complex(jnp.cos(phase_azimuth), jnp.sin(phase_azimuth))

    def focus_block(block):
        signal = lax.complex(block[0], block[1])
        signal = jnp.pad(signal, ((0, TAIL), (0, 0)))
        signal = jnp.fft.fft(signal, axis=0) * turn_one
        signal = jnp.fft.fft(signal, axis=1) * turn_two
        signal = jnp.fft.ifft(signal, axis=1) * turn_three
        signal = jnp.fft.ifft(signal, axis=0)
        return jnp.stack([jnp.real(signal), jnp.imag(signal)])

    focused = lax.map(focus_block, blocks)
    head_rows = focused[:, :, :PULSES]
    tail_rows = focused[:, :, PULSES:]
    previous = jnp.concatenate([jnp.zeros_like(tail_rows[:1]), tail_rows[:-1]], axis=0)
    head_rows = head_rows.at[:, :, :TAIL].add(previous)
    return head_rows.transpose(1, 0, 2, 3).reshape(2, N_AZ * PULSES, RANGES)
```

```python
import functools
import math

import jax
import jax.numpy as jnp
import numpy as np
from jax import lax
from jax.experimental import pallas as pl
from jax.experimental.pallas import tpu as pltpu
from jax.sharding import PartitionSpec as P

F32 = jnp.float32
BF16 = jnp.bfloat16
LANES = 128
ROW_BLOCK = 16
RADIX = 8
MEBI = 1024 * 1024
ANYWHERE = pl.BlockSpec(memory_space=pl.ANY)


def params(mebibytes=16):
    return pltpu.CompilerParams(vmem_limit_bytes=mebibytes * MEBI)


def cost():
    return pl.CostEstimate(flops=1024, bytes_accessed=1024, transcendentals=0)


def from_behind(value, axis):
    length = lax.axis_size(axis)
    return lax.ppermute(value, axis, [(i, i + 1) for i in range(length - 1)])


def exchange(value, mask):
    length = lax.axis_size("tile")
    return lax.ppermute(value, "tile", [(i, i ^ mask) for i in range(length)])


def shift(value, by):
    length = lax.axis_size("tile")
    return lax.ppermute(value, "tile", [(i, (i + by) % length) for i in range(length)])


def to_chips(pieces, arrived, last=2):
    tokens = arrived[-last] if len(arrived) >= last else []
    got = [shift(gate(piece, *tokens), 2 * k) for k, piece in enumerate(pieces) if k > 0]
    arrived.append(got)
    return [pieces[0]] + got


def gate(value, *tokens):
    return lax.optimization_barrier((value, *tokens))[0]


def split_words(value):
    high = value.astype(BF16)
    low = (value - high.astype(F32)).astype(BF16)
    return high, low


def split_table(table):
    table = table.astype(np.float32)
    high = table.astype(jnp.bfloat16)
    return high, (table - high.astype(np.float32)).astype(jnp.bfloat16)


def complex_blocks(c, s):
    return np.concatenate(
        [np.concatenate([c, -s], axis=-1), np.concatenate([s, c], axis=-1)], axis=-2
    )


def roots(residue, modulus, sign):
    angle = (residue % modulus).astype(F32) * (sign * 2.0 * math.pi / modulus)
    return jnp.cos(angle), jnp.sin(angle)


def place(offset, sizes):
    j = 0
    while offset >= sizes[j]:
        offset -= sizes[j]
        j += 1
    return offset, j


def dot(left, right):
    return jnp.dot(left, right, preferred_element_type=F32)


def times_root(value, numerator, denominator):
    re, im = value
    eighths = 8 * (numerator % denominator)
    if eighths % denominator == 0:
        octant = eighths // denominator
        half = math.sqrt(0.5)
        if octant == 0:
            return re, im
        if octant == 1:
            return (re - im) * half, (re + im) * half
        if octant == 2:
            return -im, re
        if octant == 3:
            return (re + im) * -half, (re - im) * half
        if octant == 4:
            return -re, -im
        if octant == 5:
            return (im - re) * half, (re + im) * -half
        if octant == 6:
            return im, -re
        return (re + im) * half, (im - re) * half
    angle = 2.0 * math.pi * (numerator % denominator) / denominator
    c, s = math.cos(angle), math.sin(angle)
    return re * c - im * s, re * s + im * c


def short_dft(values, sign):
    count = len(values)
    if count == 1:
        return values
    even = short_dft(values[0::2], sign)
    odd = short_dft(values[1::2], sign)
    low, high = [], []
    for k in range(count // 2):
        re, im = times_root(odd[k], sign * k, count)
        low.append((even[k][0] + re, even[k][1] + im))
        high.append((even[k][0] - re, even[k][1] - im))
    return low + high


def cos_sin(angle):
    turns = jnp.round(angle * (2.0 / math.pi))
    rest = (angle - turns * 1.57079637050628662109375) - turns * -4.37113900018624283e-8
    sq = rest * rest
    sin_r = rest + rest * sq * (-1.6666654611e-1 + sq * (8.3321608736e-3 + sq * -1.9515295891e-4))
    cos_r = 1.0 - 0.5 * sq + sq * sq * (
        4.166664568298827e-2 + sq * (-1.388731625493765e-3 + sq * 2.443315711809948e-5)
    )
    size = jnp.abs(turns)
    odd = size == 1.0
    flip = 1.0 - size
    return (
        jnp.where(odd, -turns * sin_r, flip * cos_r),
        jnp.where(odd, turns * cos_r, flip * sin_r),
    )


def turn_kernel(order_ref, phase_ref, *refs):
    cos_ref, sin_ref, column = refs[-3:]
    per = phase_ref.shape[1] // RADIX
    for lane in range(0, phase_ref.shape[2], LANES):
        column[...] = phase_ref[0, :, lane : lane + LANES]
        for a in range(RADIX):
            c, s = cos_sin(column[pl.ds(a, per, stride=RADIX), :])
            cos_ref[0, a * per : (a + 1) * per, lane : lane + LANES] = c
            sin_ref[0, a * per : (a + 1) * per, lane : lane + LANES] = s


def turns_of(phase, order, after=()):
    blocks, rows, width = phase.shape
    step = min(width, 512)
    shape = jax.ShapeDtypeStruct(phase.shape, F32)
    spec = pl.BlockSpec((1, rows, step), lambda i, j, order: (i, 0, j))
    return pl.pallas_call(
        turn_kernel,
        grid_spec=pltpu.PrefetchScalarGridSpec(
            num_scalar_prefetch=1,
            grid=(blocks, width // step),
            in_specs=[pl.BlockSpec((1, rows, step), lambda i, j, order: (order[i], 0, j))]
            + [ANYWHERE] * len(after),
            out_specs=[spec, spec],
            scratch_shapes=[pltpu.VMEM((rows, LANES), F32)],
        ),
        out_shape=[shape, shape],
        compiler_params=params(),
        cost_estimate=cost(),
        name="phase_turns",
    )(order, phase, *after)


def azimuth_front_kernel(count, place_ref, high_ref, low_ref, *refs):
    pieces, (out_ref, hi, lo) = refs[:count], refs[-3:]
    per = pieces[0].shape[1]
    half = hi.shape[0] // 2
    rows = out_ref.shape[1]
    for q in range(count):
        owner = place_ref[0] ^ q
        for part in range(2):
            top = pl.ds(pl.multiple_of(part * half + owner * per, per), per)
            hi[top, :], lo[top, :] = split_words(pieces[q][part])
    mixed = dot(high_ref[0], hi[...]) + dot(high_ref[0], lo[...]) + dot(low_ref[0], hi[...])
    out_ref[0] = mixed[:rows]
    out_ref[1] = mixed[rows:]


def azimuth_front(pieces, t, table, after=()):
    count = len(pieces)
    per, width = pieces[0].shape[1:]
    _, double, depth = table[0].shape
    step = min(width, 256)
    whole = pl.BlockSpec((1, double, depth), lambda i, t: (t[0], 0, 0))
    return pl.pallas_call(
        functools.partial(azimuth_front_kernel, count),
        grid_spec=pltpu.PrefetchScalarGridSpec(
            num_scalar_prefetch=1,
            grid=(width // step,),
            in_specs=[whole, whole]
            + [pl.BlockSpec((2, per, step), lambda i, t: (0, 0, i))] * count
            + [ANYWHERE] * len(after),
            out_specs=pl.BlockSpec((2, double // 2, step), lambda i, t: (0, 0, i)),
            scratch_shapes=[pltpu.VMEM((depth, step), BF16)] * 2,
        ),
        out_shape=jax.ShapeDtypeStruct((2, double // 2, width), F32),
        compiler_params=params(),
        cost_estimate=cost(),
        name="azimuth_front",
    )(t, *table, *pieces, *after)


def azimuth_front_table(tiles, pulses, rows, extent):
    local = np.arange(rows).reshape(rows // RADIX, RADIX).T.reshape(-1)
    doppler = np.arange(tiles)[:, None] * rows + local[None, :]
    residue = doppler[:, :, None] * np.arange(pulses) % extent
    angle = residue * (-2.0 * math.pi / extent)
    return split_table(complex_blocks(np.cos(angle), np.sin(angle)))


def sectioned_dft(load, emit, count, sign, stage_re, stage_im, rows):
    inner = min(8, count)
    outer = count // inner
    for a0 in range(outer):
        mixed = short_dft([load(outer * a1 + a0) for a1 in range(inner)], sign)
        for k in range(inner):
            re, im = times_root(mixed[k], sign * a0 * k, count)
            top = (a0 * inner + k) * rows
            stage_re[top : top + rows, :] = re
            stage_im[top : top + rows, :] = im
    for k in range(inner):
        tops = [(a0 * inner + k) * rows for a0 in range(outer)]
        mixed = short_dft(
            [(stage_re[top : top + rows, :], stage_im[top : top + rows, :]) for top in tops], sign
        )
        for m in range(outer):
            emit(k + inner * m, mixed[m])


def range_kernel(n_in, n_keep, tiles, widths, place_ref, *refs):
    refs = list(refs)
    u_refs = [refs.pop(0) for _ in range(n_in)]
    cs_ref, ss_ref, cr_ref, sr_ref, front_ref, back_ref, wf_ref, wi_ref = [
        refs.pop(0) for _ in range(8)
    ]
    del refs[:n_keep]
    outs = [[refs.pop(0) for _ in range(tiles // 2)] for _ in widths]
    core = place_ref[0] % 2
    stage_re, stage_im, hi, lo, mid = refs
    rows = stage_re.shape[0] * LANES // (cr_ref.shape[2])
    count = cr_ref.shape[2] // LANES
    per_tile = cs_ref.shape[2] // LANES

    def load(a):
        lane, j = place(a * LANES, [u.shape[2] for u in u_refs])
        u = u_refs[j]
        re, im = u[0, :, lane : lane + LANES], u[1, :, lane : lane + LANES]
        lane = (a % per_tile) * LANES
        c = cs_ref[a // per_tile, :, lane : lane + LANES]
        s = ss_ref[a // per_tile, :, lane : lane + LANES]
        return re * c - im * s, re * s + im * c

    def put(k, re, im):
        top = k * rows
        hi[top : top + rows, :LANES], lo[top : top + rows, :LANES] = split_words(re)
        hi[top : top + rows, LANES:], lo[top : top + rows, LANES:] = split_words(im)

    def emit_front(k, value):
        re, im = value
        c, s = front_ref[0, k : k + 1, :], front_ref[1, k : k + 1, :]
        put(k, re * c - im * s, re * s + im * c)

    sectioned_dft(load, emit_front, count, -1, stage_re, stage_im, rows)
    high = hi[...]
    mid[...] = dot(jnp.concatenate([high, lo[...], high], axis=1), wf_ref[...])
    for k in range(count):
        top = k * rows
        re, im = mid[top : top + rows, :LANES], mid[top : top + rows, LANES:]
        c = cr_ref[0, :, k * LANES : (k + 1) * LANES]
        s = sr_ref[0, :, k * LANES : (k + 1) * LANES]
        put(k, re * c - im * s, re * s + im * c)
    high = hi[...]
    mid[...] = dot(jnp.concatenate([high, lo[...], high], axis=1), wi_ref[...])

    def load_back(k):
        top = k * rows
        re, im = mid[top : top + rows, :LANES], mid[top : top + rows, LANES:]
        c, s = back_ref[0, k : k + 1, :], back_ref[1, k : k + 1, :]
        return re * c - im * s, re * s + im * c

    def emit_back(a, value):
        lane, j = place((a % per_tile) * LANES, widths)
        tile = a // per_tile
        out, toward = outs[j][tile // 2], (tile % 2) ^ core
        out[toward, 0, :, lane : lane + LANES] = value[0]
        out[toward, 1, :, lane : lane + LANES] = value[1]

    sectioned_dft(load_back, emit_back, count, 1, stage_re, stage_im, rows)


def range_tables(t, tiles, count):
    k = jnp.arange(count, dtype=jnp.int32)[:, None]
    b = jnp.arange(LANES, dtype=jnp.int32)[None, :]
    extent = count * LANES
    front = jnp.stack(roots(k * b, extent, -1.0))
    back = jnp.stack(roots(k * (b + t // 2 * 2 * (extent // tiles)), extent, 1.0)) * (1.0 / extent)
    return front, back


def range_mix(sign):
    index = np.arange(LANES)
    angle = (index[:, None] * index[None, :] % LANES) * (sign * 2.0 * math.pi / LANES)
    c, s = np.cos(angle), np.sin(angle)
    table = np.block([[c, s], [-s, c]]).astype(np.float32)
    high = table.astype(jnp.bfloat16)
    low = (table - high.astype(np.float32)).astype(jnp.bfloat16)
    return jnp.asarray(np.concatenate([high, high, low], axis=0))


def range_pass(spectra, t, scaling, ranging, front, back, span, split, widths, earlier, after):
    rows = spectra[0].shape[1]
    tiles, _, width = scaling[0].shape
    extent = ranging[0].shape[2]
    count = extent // LANES
    block = ROW_BLOCK
    first, steps = span
    wf, wi = range_mix(-1.0), range_mix(1.0)
    in_specs = [
        pl.BlockSpec((2, block, u.shape[2]), lambda i, t: (0, first + i, 0)) for u in spectra
    ]
    in_specs += [pl.BlockSpec((tiles, block, width), lambda i, t: (0, first + i, 0))] * 2
    in_specs += [pl.BlockSpec((1, block, extent), lambda i, t: (0, first + i, 0))] * 2
    in_specs += [pl.BlockSpec((2, count, LANES), lambda i, t: (0, 0, 0))] * 2
    in_specs += [pl.BlockSpec(wf.shape, lambda i, t: (0, 0))] * 2
    n_base = 1 + len(in_specs)
    in_specs += [ANYWHERE] * (len(earlier) + len(after))
    chips = tiles // 2
    out_specs, out_shape = [], []
    for j, out_width in enumerate(widths):
        lead = 0 if j < split else first
        out_rows = steps * block if j < split else rows
        spec = pl.BlockSpec(
            (2, 2, block, out_width), lambda i, t, lead=lead: (0, 0, lead + i, 0)
        )
        out_specs += [spec] * chips
        out_shape += [jax.ShapeDtypeStruct((2, 2, out_rows, out_width), F32)] * chips
    aliases = {n_base + i: split * chips + i for i in range(len(earlier))}
    flat = pl.pallas_call(
        functools.partial(range_kernel, len(spectra), len(earlier) + len(after), tiles, widths),
        grid_spec=pltpu.PrefetchScalarGridSpec(
            num_scalar_prefetch=1,
            grid=(steps,),
            in_specs=in_specs,
            out_specs=out_specs,
            scratch_shapes=[
                pltpu.VMEM((count * block, LANES), F32),
                pltpu.VMEM((count * block, LANES), F32),
                pltpu.VMEM((count * block, 2 * LANES), BF16),
                pltpu.VMEM((count * block, 2 * LANES), BF16),
                pltpu.VMEM((count * block, 2 * LANES), F32),
            ],
        ),
        out_shape=out_shape,
        input_output_aliases=aliases,
        compiler_params=params(),
        cost_estimate=cost(),
        name="range_filter",
    )(t, *spectra, *scaling, *ranging, front, back, wf, wi, *earlier, *after)
    return [flat[j * chips : (j + 1) * chips] for j in range(len(widths))]


def azimuth_back_kernel(layout, place_ref, high_ref, low_ref, cos_ref, sin_ref, *refs):
    total = sum(len(rows) for rows in layout)
    pieces, (head_ref, tail_ref, kbuf, z) = refs[:total], refs[-4:]
    grouped, at = [], 0
    for rows in layout:
        grouped.append(list(zip(rows, pieces[at : at + len(rows)])))
        at += len(rows)
    per = cos_ref.shape[1] // RADIX
    mixed_rows = z.shape[1] // 2
    tiles = len(layout)
    for a in range(RADIX):
        for r, group in enumerate(grouped):
            owner = lax.rem(place_ref[0] + tiles - r // 2 * 2, tiles) ^ (r % 2)
            first, low = 0, a * per
            for rows, piece in group:
                high = min((a + 1) * per, first + rows)
                if first <= low < high:
                    c, s = cos_ref[owner, low:high, :], sin_ref[owner, low:high, :]
                    re = piece[0, 0, low - first : high - first, :]
                    im = piece[0, 1, low - first : high - first, :]
                    top = pl.ds(pl.multiple_of(owner * per + low - a * per, 8), high - low)
                    kbuf[0, top, :] = re * c - im * s
                    kbuf[1, top, :] = re * s + im * c
                    low = high
                first += rows
        hi, lo = split_words(kbuf[...].reshape(z.shape[1:]))
        z[a] = dot(high_ref[a], hi) + dot(high_ref[a], lo) + dot(low_ref[a], hi)
    half = RADIX // 2
    for low in range(0, mixed_rows, 8):
        values = [
            (z[a, low : low + 8, :], z[a, mixed_rows + low : mixed_rows + low + 8, :])
            for a in range(RADIX)
        ]
        for p, value in enumerate(short_dft(values, 1)):
            ref = head_ref if p < half else tail_ref
            top = (p % half) * mixed_rows + low
            ref[0, top : top + 8, :] = value[0]
            ref[1, top : top + 8, :] = value[1]


def azimuth_back(pieces, t, turns, table, column, after=()):
    flat = [piece for group in pieces for piece in group]
    layout = [[piece.shape[2] for piece in group] for group in pieces]
    width = flat[0].shape[3]
    tiles, rows, _ = turns[0].shape
    double = table[0].shape[1]
    out_rows = RADIX * double // 4
    out = jax.ShapeDtypeStruct((2, out_rows, width), F32)
    whole = pl.BlockSpec(table[0].shape, lambda i, t: (0, 0, 0))
    turn = pl.BlockSpec((tiles, rows, width), lambda i, t: (0, 0, column // width))
    return pl.pallas_call(
        functools.partial(azimuth_back_kernel, layout),
        grid_spec=pltpu.PrefetchScalarGridSpec(
            num_scalar_prefetch=1,
            grid=(1,),
            in_specs=[whole, whole, turn, turn]
            + [pl.BlockSpec((1, *piece.shape[1:]), lambda i, t: (0, 0, 0, 0)) for piece in flat]
            + [ANYWHERE] * len(after),
            out_specs=[pl.BlockSpec((2, out_rows, width), lambda i, t: (0, 0, 0))] * 2,
            scratch_shapes=[
                pltpu.VMEM((2, double // 2, width), F32),
                pltpu.VMEM((RADIX, double, width), F32),
            ],
        ),
        out_shape=[out, out],
        compiler_params=params(24),
        cost_estimate=cost(),
        name="azimuth_back",
    )(t, *table, *turns, *flat, *after)


def azimuth_back_table(extent):
    index = np.arange(extent // RADIX)
    doppler = RADIX * index[None, :] + np.arange(RADIX)[:, None]
    residue = doppler[:, None, :] * index[None, :, None] % extent
    angle = residue * (2.0 * math.pi / extent)
    return split_table(complex_blocks(np.cos(angle), np.sin(angle)) / extent)


def add_kernel(head_ref, tail_ref, *refs):
    refs[-1][...] = head_ref[...] + tail_ref[...]


def add_tail(head, tail, earlier, column, full_width):
    _, rows, width = head.shape
    spec = pl.BlockSpec((1, rows, width), lambda i: (i, 0, 0))
    kept = [] if earlier is None else [earlier]
    return pl.pallas_call(
        add_kernel,
        grid=(2,),
        in_specs=[spec, spec] + [ANYWHERE] * len(kept),
        out_specs=pl.BlockSpec((1, rows, width), lambda i: (i, 0, column // width)),
        out_shape=jax.ShapeDtypeStruct((2, rows, full_width), F32),
        input_output_aliases={2: 0} if kept else {},
        compiler_params=params(),
        cost_estimate=cost(),
        name="add_tail",
    )(head, tail, *kept)


def scaling_cuts(phase_scaling, rows):
    tiles = lax.axis_size("tile")
    t = lax.axis_index("tile")
    copies = lax.axis_size("strip") * lax.axis_size("az")
    replica = lax.axis_index("strip") * lax.axis_size("az") + lax.axis_index("az")
    share = rows // copies

    def rows_at(start, size):
        return lax.dynamic_slice(phase_scaling, (start, 0), (size, phase_scaling.shape[1]))

    near = [rows_at((t ^ q) * rows, rows) for q in range(2)]
    far = [rows_at((t ^ q) * rows + replica * share, share) for q in range(2, tiles)]
    return near, far


def body(raw_echo, phase_scaling, phase_range, phase_azimuth):
    tiles = lax.axis_size("tile")
    t = lax.axis_index("tile")
    place_t = t.reshape(1)
    per, ranges = raw_echo.shape[1:]
    extent, width = phase_scaling.shape
    rows = phase_range.shape[0]
    count = ranges // LANES
    index = jnp.arange(tiles, dtype=jnp.int32)

    near, far = scaling_cuts(phase_scaling, rows)
    far_sent = [exchange(cut, q + 2) for q, cut in enumerate(far)]

    eighth = ranges // 8
    straight, at = [], 0
    for size in (4 * eighth, 3 * eighth, eighth):
        piece = gate(raw_echo[:, :, at : at + size], *far_sent)
        at += size
        straight.append([piece] + [exchange(piece, q) for q in range(2, tiles, 2)])

    far_all = lax.all_gather(jnp.stack(far_sent), ("strip", "az"))
    near[1] = exchange(near[1], 1)

    permuted = phase_range.reshape(rows, LANES, count).transpose(0, 2, 1).reshape(1, rows, ranges)
    ranging = turns_of(permuted, jnp.zeros((1,), jnp.int32))
    azimuth = turns_of(phase_azimuth.reshape(tiles, rows, width), index, after=[ranging[0]])
    front, back = range_tables(t, tiles, count)
    front_table = azimuth_front_table(tiles, per * tiles, rows, extent)
    back_table = azimuth_back_table(extent)

    tokens = [azimuth[0], front, back]
    spectra = []
    for j, received in enumerate(straight):
        received = [gate(piece, *tokens) for piece in received]
        handed = [exchange(piece, 1) for piece in received]
        got = [piece for pair in zip(received, handed) for piece in pair]
        spectra.append(azimuth_front(got, place_t, front_table))
        tokens = [spectra[-1]]
        if j == 0:
            far_rows = gate(far_all, *tokens).transpose(1, 0, 2, 3)
            far_rows = far_rows.reshape(tiles - 2, rows, width)
            pieces = jnp.concatenate([near[0][None], near[1][None], far_rows])
            scaling = turns_of(pieces, t ^ index)
            tokens = [scaling[0]]

    if width >= 8 * LANES:
        widths = [width // 4] * 3 + [width // 8] * 2
    else:
        widths = [LANES] * (width // LANES)
    blocks = rows // ROW_BLOCK
    spans = [(0, blocks)] if blocks < 16 else [(0, blocks // 2), (blocks // 2, blocks // 2)]
    split = 1 if len(spans) > 1 else 0
    parts, kept, sequence = [], [], []
    for span in spans:
        done = range_pass(
            spectra, place_t, scaling, ranging, front, back, span, split, widths, kept, []
        )
        parts.append([to_chips(chunk, sequence, 1) for chunk in done[:split]])
        kept = [piece for chunk in done[split:] for piece in chunk]
    arrived = [[part[j] for part in parts] for j in range(split)]
    for j, chunk in enumerate(done[split:]):
        arrived.append([to_chips(chunk, sequence, 1 if j == 0 else 2)])

    heads, tails, images, column = [], [], [], 0
    for j, groups in enumerate(arrived):
        groups = [[gate(piece, *heads[-1:]) for piece in group] for group in groups]
        pieces = []
        for k in range(tiles // 2):
            pieces.append([group[k] for group in groups])
            pieces.append([exchange(group[k][1:], 1) for group in groups])
        before = heads[-1:]
        head, tail = azimuth_back(pieces, place_t, azimuth, back_table, column, after=before)
        heads.append(head)
        tokens = [tails[-1][0]] if tails else []
        tails.append((from_behind(gate(tail, *tokens), "az"), column))
        column += widths[j]
        if j >= 2:
            tail, at = tails[j - 2]
            image = images[-1] if images else None
            images.append(add_tail(heads[j - 2], tail, image, at, width))
    for j in range(len(images), len(heads)):
        tail, at = tails[j]
        images.append(add_tail(heads[j], tail, images[-1] if images else None, at, width))
    return images[-1]


def solution(mesh):
    return jax.shard_map(
        body,
        mesh=mesh,
        in_specs=(
            P(None, ("strip", "az", "tile"), None),
            P(None, "tile"),
            P("tile", None),
            P(None, "tile"),
        ),
        out_specs=P(None, ("strip", "az"), "tile"),
        check_vma=False,
    )
```

```python
import functools
import math

import jax
import jax.numpy as jnp
import numpy as np
from jax import lax
from jax.experimental import pallas as pl
from jax.experimental.pallas import tpu as pltpu
from jax.sharding import PartitionSpec as P

F32 = jnp.float32
BF16 = jnp.bfloat16
LANES = 128
ROW_BLOCK = 32
PART_ROWS = 16
RADIX = 8
MEBI = 1024 * 1024
ANYWHERE = pl.BlockSpec(memory_space=pl.ANY)


def params(mebibytes=16):
    return pltpu.CompilerParams(vmem_limit_bytes=mebibytes * MEBI)


def cost():
    return pl.CostEstimate(flops=1024, bytes_accessed=1024, transcendentals=0)


def from_behind(value, axis):
    length = lax.axis_size(axis)
    return lax.ppermute(value, axis, [(i, i + 1) for i in range(length - 1)])


def exchange(value, mask):
    length = lax.axis_size("tile")
    return lax.ppermute(value, "tile", [(i, i ^ mask) for i in range(length)])


def shift(value, by):
    length = lax.axis_size("tile")
    return lax.ppermute(value, "tile", [(i, (i + by) % length) for i in range(length)])


def to_chips(pieces, arrived, last=2):
    tokens = arrived[-last] if len(arrived) >= last else []
    got = [shift(gate(piece, *tokens), 2 * k) for k, piece in enumerate(pieces) if k > 0]
    arrived.append(got)
    return [pieces[0]] + got


def gate(value, *tokens):
    return lax.optimization_barrier((value, *tokens))[0]


def split_words(value):
    high = value.astype(BF16)
    low = (value - high.astype(F32)).astype(BF16)
    return high, low


def split_table(table):
    table = table.astype(np.float32)
    high = table.astype(jnp.bfloat16)
    return high, (table - high.astype(np.float32)).astype(jnp.bfloat16)


def complex_blocks(c, s):
    return np.concatenate(
        [np.concatenate([c, -s], axis=-1), np.concatenate([s, c], axis=-1)], axis=-2
    )


def roots(residue, modulus, sign):
    angle = (residue % modulus).astype(F32) * (sign * 2.0 * math.pi / modulus)
    return jnp.cos(angle), jnp.sin(angle)


def place(offset, sizes):
    j = 0
    while offset >= sizes[j]:
        offset -= sizes[j]
        j += 1
    return offset, j


def dot(left, right):
    return jnp.dot(left, right, preferred_element_type=F32)


def times_root(value, numerator, denominator):
    re, im = value
    eighths = 8 * (numerator % denominator)
    if eighths % denominator == 0:
        octant = eighths // denominator
        half = math.sqrt(0.5)
        if octant == 0:
            return re, im
        if octant == 1:
            return (re - im) * half, (re + im) * half
        if octant == 2:
            return -im, re
        if octant == 3:
            return (re + im) * -half, (re - im) * half
        if octant == 4:
            return -re, -im
        if octant == 5:
            return (im - re) * half, (re + im) * -half
        if octant == 6:
            return im, -re
        return (re + im) * half, (im - re) * half
    angle = 2.0 * math.pi * (numerator % denominator) / denominator
    c, s = math.cos(angle), math.sin(angle)
    return re * c - im * s, re * s + im * c


def short_dft(values, sign):
    count = len(values)
    if count == 1:
        return values
    even = short_dft(values[0::2], sign)
    odd = short_dft(values[1::2], sign)
    low, high = [], []
    for k in range(count // 2):
        re, im = times_root(odd[k], sign * k, count)
        low.append((even[k][0] + re, even[k][1] + im))
        high.append((even[k][0] - re, even[k][1] - im))
    return low + high


def cos_sin(angle):
    turns = jnp.round(angle * (2.0 / math.pi))
    rest = (angle - turns * 1.57079637050628662109375) - turns * -4.37113900018624283e-8
    sq = rest * rest
    sin_r = rest + rest * sq * (-1.6666654611e-1 + sq * (8.3321608736e-3 + sq * -1.9515295891e-4))
    cos_r = 1.0 - 0.5 * sq + sq * sq * (
        4.166664568298827e-2 + sq * (-1.388731625493765e-3 + sq * 2.443315711809948e-5)
    )
    size = jnp.abs(turns)
    odd = size == 1.0
    flip = 1.0 - size
    return (
        jnp.where(odd, -turns * sin_r, flip * cos_r),
        jnp.where(odd, turns * cos_r, flip * sin_r),
    )


def turn_kernel(order_ref, phase_ref, *refs):
    cos_ref, sin_ref, column = refs[-3:]
    per = phase_ref.shape[1] // RADIX
    for lane in range(0, phase_ref.shape[2], LANES):
        column[...] = phase_ref[0, :, lane : lane + LANES]
        for a in range(RADIX):
            c, s = cos_sin(column[pl.ds(a, per, stride=RADIX), :])
            cos_ref[0, a * per : (a + 1) * per, lane : lane + LANES] = c
            sin_ref[0, a * per : (a + 1) * per, lane : lane + LANES] = s


def turns_of(phase, order, after=()):
    blocks, rows, width = phase.shape
    step = min(width, 512)
    shape = jax.ShapeDtypeStruct(phase.shape, F32)
    spec = pl.BlockSpec((1, rows, step), lambda i, j, order: (i, 0, j))
    return pl.pallas_call(
        turn_kernel,
        grid_spec=pltpu.PrefetchScalarGridSpec(
            num_scalar_prefetch=1,
            grid=(blocks, width // step),
            in_specs=[pl.BlockSpec((1, rows, step), lambda i, j, order: (order[i], 0, j))]
            + [ANYWHERE] * len(after),
            out_specs=[spec, spec],
            scratch_shapes=[pltpu.VMEM((rows, LANES), F32)],
        ),
        out_shape=[shape, shape],
        compiler_params=params(),
        cost_estimate=cost(),
        name="phase_turns",
    )(order, phase, *after)


def azimuth_front_kernel(count, place_ref, high_ref, low_ref, cos_ref, sin_ref, *refs):
    pieces, (out_ref, hi, lo) = refs[:count], refs[-3:]
    per = pieces[0].shape[1]
    half = hi.shape[0] // 2
    rows = out_ref.shape[1]
    for q in range(count):
        owner = place_ref[0] ^ q
        for part in range(2):
            top = pl.ds(pl.multiple_of(part * half + owner * per, per), per)
            hi[top, :], lo[top, :] = split_words(pieces[q][part])
    mixed = dot(high_ref[0], hi[...]) + dot(high_ref[0], lo[...]) + dot(low_ref[0], hi[...])
    re, im = mixed[:rows], mixed[rows:]
    c, s = cos_ref[0], sin_ref[0]
    out_ref[0] = re * c - im * s
    out_ref[1] = re * s + im * c


def azimuth_front(pieces, t, table, scaling, column):
    count = len(pieces)
    per, width = pieces[0].shape[1:]
    _, double, depth = table[0].shape
    step = min(256, scaling[0].shape[2])
    per_tile = scaling[0].shape[2] // step
    first = column // step
    whole = pl.BlockSpec((1, double, depth), lambda i, t: (t[0], 0, 0))
    turn = pl.BlockSpec(
        (1, double // 2, step), lambda i, t: ((first + i) // per_tile, 0, (first + i) % per_tile)
    )
    return pl.pallas_call(
        functools.partial(azimuth_front_kernel, count),
        grid_spec=pltpu.PrefetchScalarGridSpec(
            num_scalar_prefetch=1,
            grid=(width // step,),
            in_specs=[whole, whole, turn, turn]
            + [pl.BlockSpec((2, per, step), lambda i, t: (0, 0, i))] * count,
            out_specs=pl.BlockSpec((2, double // 2, step), lambda i, t: (0, 0, i)),
            scratch_shapes=[pltpu.VMEM((depth, step), BF16)] * 2,
        ),
        out_shape=jax.ShapeDtypeStruct((2, double // 2, width), F32),
        compiler_params=params(),
        cost_estimate=cost(),
        name="azimuth_front",
    )(t, *table, *scaling, *pieces)


def azimuth_front_table(tiles, pulses, rows, extent):
    local = np.arange(rows).reshape(rows // RADIX, RADIX).T.reshape(-1)
    doppler = np.arange(tiles)[:, None] * rows + local[None, :]
    residue = doppler[:, :, None] * np.arange(pulses) % extent
    angle = residue * (-2.0 * math.pi / extent)
    return split_table(complex_blocks(np.cos(angle), np.sin(angle)))


def sectioned_dft(load, emit, count, sign, stage_re, stage_im, rows):
    inner = min(8, count)
    outer = count // inner
    for a0 in range(outer):
        mixed = short_dft([load(outer * a1 + a0) for a1 in range(inner)], sign)
        for k in range(inner):
            re, im = times_root(mixed[k], sign * a0 * k, count)
            top = (a0 * inner + k) * rows
            stage_re[top : top + rows, :] = re
            stage_im[top : top + rows, :] = im
    for k in range(inner):
        tops = [(a0 * inner + k) * rows for a0 in range(outer)]
        mixed = short_dft(
            [(stage_re[top : top + rows, :], stage_im[top : top + rows, :]) for top in tops], sign
        )
        for m in range(outer):
            emit(k + inner * m, mixed[m])


def range_kernel(n_in, n_keep, tiles, widths, place_ref, *refs):
    refs = list(refs)
    u_refs = [refs.pop(0) for _ in range(n_in)]
    cr_ref, sr_ref, front_ref, back_ref, wf_ref, wi_ref = [refs.pop(0) for _ in range(6)]
    del refs[:n_keep]
    outs = [[refs.pop(0) for _ in range(tiles // 2)] for _ in widths]
    core = place_ref[0] % 2
    parts = len(refs) // 5
    rows = u_refs[0].shape[1] // parts
    count = cr_ref.shape[2] // LANES
    per_tile = count // tiles
    sizes = [u.shape[2] for u in u_refs]

    def steps_of(part):
        stage_re, stage_im, hi, lo, mid = refs[5 * part : 5 * part + 5]
        here = slice(part * rows, (part + 1) * rows)

        def load(a):
            lane, j = place(a * LANES, sizes)
            u = u_refs[j]
            return u[0, here, lane : lane + LANES], u[1, here, lane : lane + LANES]

        def put(k, re, im):
            top = k * rows
            hi[top : top + rows, :LANES], lo[top : top + rows, :LANES] = split_words(re)
            hi[top : top + rows, LANES:], lo[top : top + rows, LANES:] = split_words(im)

        def emit_front(k, value):
            re, im = value
            c, s = front_ref[0, k : k + 1, :], front_ref[1, k : k + 1, :]
            put(k, re * c - im * s, re * s + im * c)

        def front():
            sectioned_dft(load, emit_front, count, -1, stage_re, stage_im, rows)

        def mix(table_ref):
            high = hi[...]
            mid[...] = dot(jnp.concatenate([high, lo[...], high], axis=1), table_ref[...])

        def filtered():
            for k in range(count):
                top = k * rows
                re, im = mid[top : top + rows, :LANES], mid[top : top + rows, LANES:]
                c = cr_ref[0, here, k * LANES : (k + 1) * LANES]
                s = sr_ref[0, here, k * LANES : (k + 1) * LANES]
                put(k, re * c - im * s, re * s + im * c)

        def load_back(k):
            top = k * rows
            re, im = mid[top : top + rows, :LANES], mid[top : top + rows, LANES:]
            c, s = back_ref[0, k : k + 1, :], back_ref[1, k : k + 1, :]
            return re * c - im * s, re * s + im * c

        def emit_back(a, value):
            lane, j = place((a % per_tile) * LANES, widths)
            tile = a // per_tile
            out, toward = outs[j][tile // 2], (tile % 2) ^ core
            out[toward, 0, here, lane : lane + LANES] = value[0]
            out[toward, 1, here, lane : lane + LANES] = value[1]

        def back():
            sectioned_dft(load_back, emit_back, count, 1, stage_re, stage_im, rows)

        return [front, lambda: mix(wf_ref), filtered, lambda: mix(wi_ref), back]

    work = [steps_of(part) for part in range(parts)]
    for at in range(5 + 2 * parts):
        for part in range(parts):
            if 0 <= at - part < 5:
                work[part][at - part]()


def range_tables(t, tiles, count):
    k = jnp.arange(count, dtype=jnp.int32)[:, None]
    b = jnp.arange(LANES, dtype=jnp.int32)[None, :]
    extent = count * LANES
    front = jnp.stack(roots(k * b, extent, -1.0))
    back = jnp.stack(roots(k * (b + t // 2 * 2 * (extent // tiles)), extent, 1.0)) * (1.0 / extent)
    return front, back


def range_mix(sign):
    index = np.arange(LANES)
    angle = (index[:, None] * index[None, :] % LANES) * (sign * 2.0 * math.pi / LANES)
    c, s = np.cos(angle), np.sin(angle)
    table = np.block([[c, s], [-s, c]]).astype(np.float32)
    high = table.astype(jnp.bfloat16)
    low = (table - high.astype(np.float32)).astype(jnp.bfloat16)
    return jnp.asarray(np.concatenate([high, high, low], axis=0))


def range_pass(spectra, t, tiles, ranging, front, back, span, split, widths, earlier, after):
    rows = spectra[0].shape[1]
    extent = ranging[0].shape[2]
    count = extent // LANES
    block = ROW_BLOCK
    first, steps = span
    wf, wi = range_mix(-1.0), range_mix(1.0)
    in_specs = [
        pl.BlockSpec((2, block, u.shape[2]), lambda i, t: (0, first + i, 0)) for u in spectra
    ]
    in_specs += [pl.BlockSpec((1, block, extent), lambda i, t: (0, first + i, 0))] * 2
    in_specs += [pl.BlockSpec((2, count, LANES), lambda i, t: (0, 0, 0))] * 2
    in_specs += [pl.BlockSpec(wf.shape, lambda i, t: (0, 0))] * 2
    n_base = 1 + len(in_specs)
    in_specs += [ANYWHERE] * (len(earlier) + len(after))
    chips = tiles // 2
    out_specs, out_shape = [], []
    for j, out_width in enumerate(widths):
        lead = 0 if j < split else first
        out_rows = steps * block if j < split else rows
        spec = pl.BlockSpec(
            (2, 2, block, out_width), lambda i, t, lead=lead: (0, 0, lead + i, 0)
        )
        out_specs += [spec] * chips
        out_shape += [jax.ShapeDtypeStruct((2, 2, out_rows, out_width), F32)] * chips
    aliases = {n_base + i: split * chips + i for i in range(len(earlier))}
    flat = pl.pallas_call(
        functools.partial(range_kernel, len(spectra), len(earlier) + len(after), tiles, widths),
        grid_spec=pltpu.PrefetchScalarGridSpec(
            num_scalar_prefetch=1,
            grid=(steps,),
            in_specs=in_specs,
            out_specs=out_specs,
            scratch_shapes=[
                pltpu.VMEM((count * PART_ROWS, LANES), F32),
                pltpu.VMEM((count * PART_ROWS, LANES), F32),
                pltpu.VMEM((count * PART_ROWS, 2 * LANES), BF16),
                pltpu.VMEM((count * PART_ROWS, 2 * LANES), BF16),
                pltpu.VMEM((count * PART_ROWS, 2 * LANES), F32),
            ]
            * (block // PART_ROWS),
        ),
        out_shape=out_shape,
        input_output_aliases=aliases,
        compiler_params=params(),
        cost_estimate=cost(),
        name="range_filter",
    )(t, *spectra, *ranging, front, back, wf, wi, *earlier, *after)
    return [flat[j * chips : (j + 1) * chips] for j in range(len(widths))]


def azimuth_back_kernel(layout, place_ref, high_ref, low_ref, cos_ref, sin_ref, *refs):
    total = sum(len(rows) for rows in layout)
    pieces, (head_ref, tail_ref, kbuf, z) = refs[:total], refs[-4:]
    grouped, at = [], 0
    for rows in layout:
        grouped.append(list(zip(rows, pieces[at : at + len(rows)])))
        at += len(rows)
    per = cos_ref.shape[1] // RADIX
    mixed_rows = z.shape[1] // 2
    tiles = len(layout)
    for a in range(RADIX):
        for r, group in enumerate(grouped):
            owner = lax.rem(place_ref[0] + tiles - r // 2 * 2, tiles) ^ (r % 2)
            first, low = 0, a * per
            for rows, piece in group:
                high = min((a + 1) * per, first + rows)
                if first <= low < high:
                    c, s = cos_ref[owner, low:high, :], sin_ref[owner, low:high, :]
                    re = piece[0, 0, low - first : high - first, :]
                    im = piece[0, 1, low - first : high - first, :]
                    top = pl.ds(pl.multiple_of(owner * per + low - a * per, 8), high - low)
                    kbuf[0, top, :] = re * c - im * s
                    kbuf[1, top, :] = re * s + im * c
                    low = high
                first += rows
        hi, lo = split_words(kbuf[...].reshape(z.shape[1:]))
        z[a] = dot(high_ref[a], hi) + dot(high_ref[a], lo) + dot(low_ref[a], hi)
    half = RADIX // 2
    for low in range(0, mixed_rows, 8):
        values = [
            (z[a, low : low + 8, :], z[a, mixed_rows + low : mixed_rows + low + 8, :])
            for a in range(RADIX)
        ]
        for p, value in enumerate(short_dft(values, 1)):
            top = (p % half) * mixed_rows + low
            ref = head_ref if p < half else tail_ref
            ref[0, top : top + 8, :] = value[0]
            ref[1, top : top + 8, :] = value[1]


def azimuth_back(pieces, t, turns, table, column, after=()):
    flat = [piece for group in pieces for piece in group]
    layout = [[piece.shape[2] for piece in group] for group in pieces]
    width = flat[0].shape[3]
    tiles, rows, _ = turns[0].shape
    double = table[0].shape[1]
    outs = [jax.ShapeDtypeStruct((2, RADIX * double // 4, width), F32)] * 2
    whole = pl.BlockSpec(table[0].shape, lambda i, t: (0, 0, 0))
    turn = pl.BlockSpec((tiles, rows, width), lambda i, t: (0, 0, column // width))
    return pl.pallas_call(
        functools.partial(azimuth_back_kernel, layout),
        grid_spec=pltpu.PrefetchScalarGridSpec(
            num_scalar_prefetch=1,
            grid=(1,),
            in_specs=[whole, whole, turn, turn]
            + [pl.BlockSpec((1, *piece.shape[1:]), lambda i, t: (0, 0, 0, 0)) for piece in flat]
            + [ANYWHERE] * len(after),
            out_specs=[pl.BlockSpec(out.shape, lambda i, t: (0, 0, 0)) for out in outs],
            scratch_shapes=[
                pltpu.VMEM((2, double // 2, width), F32),
                pltpu.VMEM((RADIX, double, width), F32),
            ],
        ),
        out_shape=outs,
        compiler_params=params(24),
        cost_estimate=cost(),
        name="azimuth_back",
    )(t, *table, *turns, *flat, *after)


def azimuth_back_table(extent):
    index = np.arange(extent // RADIX)
    doppler = RADIX * index[None, :] + np.arange(RADIX)[:, None]
    residue = doppler[:, None, :] * index[None, :, None] % extent
    angle = residue * (2.0 * math.pi / extent)
    return split_table(complex_blocks(np.cos(angle), np.sin(angle)) / extent)


def add_kernel(head_ref, tail_ref, *refs):
    refs[-1][...] = head_ref[...] + tail_ref[...]


def add_tail(head, tail, earlier, column, full_width):
    _, rows, width = head.shape
    kept = [] if earlier is None else [earlier]
    return pl.pallas_call(
        add_kernel,
        grid=(1,),
        in_specs=[pl.BlockSpec((2, rows, width), lambda i: (0, 0, 0))] * 2
        + [ANYWHERE] * len(kept),
        out_specs=pl.BlockSpec((2, rows, width), lambda i: (0, 0, column // width)),
        out_shape=jax.ShapeDtypeStruct((2, rows, full_width), F32),
        input_output_aliases={2: 0} if kept else {},
        compiler_params=params(),
        cost_estimate=cost(),
        name="add_tail",
    )(head, tail, *kept)


def scaling_cuts(phase_scaling, rows):
    tiles = lax.axis_size("tile")
    t = lax.axis_index("tile")
    copies = lax.axis_size("strip") * lax.axis_size("az")
    replica = lax.axis_index("strip") * lax.axis_size("az") + lax.axis_index("az")
    share = rows // copies

    def rows_at(start, size):
        return lax.dynamic_slice(phase_scaling, (start, 0), (size, phase_scaling.shape[1]))

    near = [rows_at((t ^ q) * rows, rows) for q in range(2)]
    far = [rows_at((t ^ q) * rows + replica * share, share) for q in range(2, tiles)]
    return near, far


def halves(piece):
    rows = piece.shape[2]
    cut = rows // 2 if rows >= 256 else rows
    return [piece[1:, :, low : low + cut] for low in range(0, rows, cut)]


def body(raw_echo, phase_scaling, phase_range, phase_azimuth):
    tiles = lax.axis_size("tile")
    t = lax.axis_index("tile")
    place_t = t.reshape(1)
    per, ranges = raw_echo.shape[1:]
    extent, width = phase_scaling.shape
    rows = phase_range.shape[0]
    count = ranges // LANES
    index = jnp.arange(tiles, dtype=jnp.int32)

    near, far = scaling_cuts(phase_scaling, rows)
    far_sent = [exchange(cut, q + 2) for q, cut in enumerate(far)]

    part = ranges // 8
    straight, at = [], 0
    for size in (4 * part, 3 * part, part):
        piece = gate(raw_echo[:, :, at : at + size], *far_sent)
        at += size
        straight.append([piece] + [exchange(piece, q) for q in range(2, tiles, 2)])

    far_all = lax.all_gather(jnp.stack(far_sent), ("strip", "az"))
    near[1] = exchange(near[1], 1)

    permuted = phase_range.reshape(rows, LANES, count).transpose(0, 2, 1).reshape(1, rows, ranges)
    ranging = turns_of(permuted, jnp.zeros((1,), jnp.int32))
    azimuth = turns_of(phase_azimuth.reshape(tiles, rows, width), index, after=[ranging[0]])
    front, back = range_tables(t, tiles, count)
    front_table = azimuth_front_table(tiles, per * tiles, rows, extent)
    back_table = azimuth_back_table(extent)

    tokens = [azimuth[0], front, back]
    far_rows = gate(far_all, *tokens).transpose(1, 0, 2, 3).reshape(tiles - 2, rows, width)
    pieces = jnp.concatenate([near[0][None], near[1][None], far_rows])
    scaling = turns_of(pieces, t ^ index, after=[azimuth[0]])
    spectra, column = [], 0
    for received in straight:
        received = [gate(piece, *tokens) for piece in received]
        handed = [exchange(piece, 1) for piece in received]
        got = [piece for pair in zip(received, handed) for piece in pair]
        spectra.append(azimuth_front(got, place_t, front_table, scaling, column))
        column += received[0].shape[2]
        tokens = [spectra[-1]]

    if width >= 8 * LANES:
        widths = [width // 4] * 4
    else:
        widths = [LANES] * (width // LANES)
    blocks = rows // ROW_BLOCK
    spans = [(0, blocks)] if blocks < 8 else [(0, blocks // 2), (blocks // 2, blocks // 2)]
    split = 1 if len(spans) > 1 else 0
    parts, kept, sequence = [], [], []
    for span in spans:
        done = range_pass(
            spectra, place_t, tiles, ranging, front, back, span, split, widths, kept, []
        )
        parts.append([to_chips(chunk, sequence, 1) for chunk in done[:split]])
        kept = [piece for chunk in done[split:] for piece in chunk]
    ready = [[part[j] for part in parts] for j in range(split)]
    for j, chunk in enumerate(done[split:]):
        ready.append([to_chips(chunk, sequence, min(j + 1, 2))])

    heads, tails, images, column = [], [], [], 0
    for j in range(len(widths)):
        tokens = heads[-1:] + tails[j - 2 : j - 1] if j >= 2 else heads[-1:]
        groups = [[gate(piece, *tokens) for piece in group] for group in ready[j]]
        pieces = []
        for k in range(tiles // 2):
            pieces.append([group[k] for group in groups])
            pieces.append([exchange(part, 1) for group in groups for part in halves(group[k])])
        head, tail = azimuth_back(
            pieces, place_t, azimuth, back_table, column, after=heads[-1:]
        )
        heads.append(head)
        tokens = tails[-1:] if j == len(widths) - 1 else []
        tails.append(from_behind(gate(tail, *tokens), "az"))
        if j >= 1:
            image = images[-1] if images else None
            images.append(
                add_tail(heads[j - 1], tails[j - 1], image, column - widths[j - 1], width)
            )
        column += widths[j]
    image = images[-1] if images else None
    return add_tail(heads[-1], tails[-1], image, column - widths[-1], width)


def solution(mesh):
    return jax.shard_map(
        body,
        mesh=mesh,
        in_specs=(
            P(None, ("strip", "az", "tile"), None),
            P(None, "tile"),
            P("tile", None),
            P(None, "tile"),
        ),
        out_specs=P(None, ("strip", "az"), "tile"),
        check_vma=False,
    )
```

```python
import functools
import math

import jax
import jax.numpy as jnp
import numpy as np
from jax import lax
from jax.experimental import pallas as pl
from jax.experimental.pallas import tpu as pltpu
from jax.sharding import PartitionSpec as P

F32 = jnp.float32
BF16 = jnp.bfloat16
LANES = 128
ROW_BLOCK = 32
PART_ROWS = 16
RADIX = 8
MEBI = 1024 * 1024
ANYWHERE = pl.BlockSpec(memory_space=pl.ANY)


def params(mebibytes=16):
    return pltpu.CompilerParams(vmem_limit_bytes=mebibytes * MEBI)


def cost():
    return pl.CostEstimate(flops=1024, bytes_accessed=1024, transcendentals=0)


def from_behind(value, axis):
    length = lax.axis_size(axis)
    return lax.ppermute(value, axis, [(i, i + 1) for i in range(length - 1)])


def exchange(value, mask):
    length = lax.axis_size("tile")
    return lax.ppermute(value, "tile", [(i, i ^ mask) for i in range(length)])


def shift(value, by):
    length = lax.axis_size("tile")
    return lax.ppermute(value, "tile", [(i, (i + by) % length) for i in range(length)])


def to_chips(pieces, arrived, last=2):
    tokens = arrived[-last] if len(arrived) >= last else []
    got = [shift(gate(piece, *tokens), 2 * k) for k, piece in enumerate(pieces) if k > 0]
    arrived.append(got)
    return [pieces[0]] + got


def gate(value, *tokens):
    return lax.optimization_barrier((value, *tokens))[0]


def split_words(value):
    high = value.astype(BF16)
    low = (value - high.astype(F32)).astype(BF16)
    return high, low


def split_table(table):
    table = table.astype(np.float32)
    high = table.astype(jnp.bfloat16)
    return high, (table - high.astype(np.float32)).astype(jnp.bfloat16)


def complex_blocks(c, s):
    return np.concatenate(
        [np.concatenate([c, -s], axis=-1), np.concatenate([s, c], axis=-1)], axis=-2
    )


def roots(residue, modulus, sign):
    angle = (residue % modulus).astype(F32) * (sign * 2.0 * math.pi / modulus)
    return jnp.cos(angle), jnp.sin(angle)


def place(offset, sizes):
    j = 0
    while offset >= sizes[j]:
        offset -= sizes[j]
        j += 1
    return offset, j


def dot(left, right):
    return jnp.dot(left, right, preferred_element_type=F32)


def times_root(value, numerator, denominator):
    re, im = value
    eighths = 8 * (numerator % denominator)
    if eighths % denominator == 0:
        octant = eighths // denominator
        half = math.sqrt(0.5)
        if octant == 0:
            return re, im
        if octant == 1:
            return (re - im) * half, (re + im) * half
        if octant == 2:
            return -im, re
        if octant == 3:
            return (re + im) * -half, (re - im) * half
        if octant == 4:
            return -re, -im
        if octant == 5:
            return (im - re) * half, (re + im) * -half
        if octant == 6:
            return im, -re
        return (re + im) * half, (im - re) * half
    angle = 2.0 * math.pi * (numerator % denominator) / denominator
    c, s = math.cos(angle), math.sin(angle)
    return re * c - im * s, re * s + im * c


def short_dft(values, sign):
    count = len(values)
    if count == 1:
        return values
    even = short_dft(values[0::2], sign)
    odd = short_dft(values[1::2], sign)
    low, high = [], []
    for k in range(count // 2):
        re, im = times_root(odd[k], sign * k, count)
        low.append((even[k][0] + re, even[k][1] + im))
        high.append((even[k][0] - re, even[k][1] - im))
    return low + high


def cos_sin(angle):
    turns = jnp.round(angle * (2.0 / math.pi))
    rest = (angle - turns * 1.57079637050628662109375) - turns * -4.37113900018624283e-8
    sq = rest * rest
    sin_r = rest + rest * sq * (-1.6666654611e-1 + sq * (8.3321608736e-3 + sq * -1.9515295891e-4))
    cos_r = 1.0 - 0.5 * sq + sq * sq * (
        4.166664568298827e-2 + sq * (-1.388731625493765e-3 + sq * 2.443315711809948e-5)
    )
    size = jnp.abs(turns)
    odd = size == 1.0
    flip = 1.0 - size
    return (
        jnp.where(odd, -turns * sin_r, flip * cos_r),
        jnp.where(odd, turns * cos_r, flip * sin_r),
    )


def turn_kernel(order_ref, phase_ref, *refs):
    cos_ref, sin_ref, column = refs[-3:]
    per = phase_ref.shape[1] // RADIX
    for lane in range(0, phase_ref.shape[2], LANES):
        column[...] = phase_ref[0, :, lane : lane + LANES]
        for a in range(RADIX):
            c, s = cos_sin(column[pl.ds(a, per, stride=RADIX), :])
            cos_ref[0, a * per : (a + 1) * per, lane : lane + LANES] = c
            sin_ref[0, a * per : (a + 1) * per, lane : lane + LANES] = s


def turns_of(phase, order, after=()):
    blocks, rows, width = phase.shape
    step = min(width, 512)
    shape = jax.ShapeDtypeStruct(phase.shape, F32)
    spec = pl.BlockSpec((1, rows, step), lambda i, j, order: (i, 0, j))
    return pl.pallas_call(
        turn_kernel,
        grid_spec=pltpu.PrefetchScalarGridSpec(
            num_scalar_prefetch=1,
            grid=(blocks, width // step),
            in_specs=[pl.BlockSpec((1, rows, step), lambda i, j, order: (order[i], 0, j))]
            + [ANYWHERE] * len(after),
            out_specs=[spec, spec],
            scratch_shapes=[pltpu.VMEM((rows, LANES), F32)],
        ),
        out_shape=[shape, shape],
        compiler_params=params(),
        cost_estimate=cost(),
        name="phase_turns",
    )(order, phase, *after)


def azimuth_front_kernel(count, place_ref, high_ref, low_ref, cos_ref, sin_ref, *refs):
    pieces, (out_ref, hi, lo) = refs[:count], refs[-3:]
    per = pieces[0].shape[1]
    half = hi.shape[0] // 2
    rows = out_ref.shape[1]
    for q in range(count):
        owner = place_ref[0] ^ q
        for part in range(2):
            top = pl.ds(pl.multiple_of(part * half + owner * per, per), per)
            hi[top, :], lo[top, :] = split_words(pieces[q][part])
    mixed = dot(high_ref[0], hi[...]) + dot(high_ref[0], lo[...]) + dot(low_ref[0], hi[...])
    re, im = mixed[:rows], mixed[rows:]
    c, s = cos_ref[0], sin_ref[0]
    out_ref[0] = re * c - im * s
    out_ref[1] = re * s + im * c


def azimuth_front(pieces, t, table, scaling, column):
    count = len(pieces)
    per, width = pieces[0].shape[1:]
    _, double, depth = table[0].shape
    step = min(256, scaling[0].shape[2])
    per_tile = scaling[0].shape[2] // step
    first = column // step
    whole = pl.BlockSpec((1, double, depth), lambda i, t: (t[0], 0, 0))
    turn = pl.BlockSpec(
        (1, double // 2, step), lambda i, t: ((first + i) // per_tile, 0, (first + i) % per_tile)
    )
    return pl.pallas_call(
        functools.partial(azimuth_front_kernel, count),
        grid_spec=pltpu.PrefetchScalarGridSpec(
            num_scalar_prefetch=1,
            grid=(width // step,),
            in_specs=[whole, whole, turn, turn]
            + [pl.BlockSpec((2, per, step), lambda i, t: (0, 0, i))] * count,
            out_specs=pl.BlockSpec((2, double // 2, step), lambda i, t: (0, 0, i)),
            scratch_shapes=[pltpu.VMEM((depth, step), BF16)] * 2,
        ),
        out_shape=jax.ShapeDtypeStruct((2, double // 2, width), F32),
        compiler_params=params(),
        cost_estimate=cost(),
        name="azimuth_front",
    )(t, *table, *scaling, *pieces)


def azimuth_front_table(tiles, pulses, rows, extent):
    local = np.arange(rows).reshape(rows // RADIX, RADIX).T.reshape(-1)
    doppler = np.arange(tiles)[:, None] * rows + local[None, :]
    residue = doppler[:, :, None] * np.arange(pulses) % extent
    angle = residue * (-2.0 * math.pi / extent)
    return split_table(complex_blocks(np.cos(angle), np.sin(angle)))


def sectioned_dft(load, emit, count, sign, stage_re, stage_im, rows):
    inner = min(8, count)
    outer = count // inner
    for a0 in range(outer):
        mixed = short_dft([load(outer * a1 + a0) for a1 in range(inner)], sign)
        for k in range(inner):
            re, im = times_root(mixed[k], sign * a0 * k, count)
            top = (a0 * inner + k) * rows
            stage_re[top : top + rows, :] = re
            stage_im[top : top + rows, :] = im
    for k in range(inner):
        tops = [(a0 * inner + k) * rows for a0 in range(outer)]
        mixed = short_dft(
            [(stage_re[top : top + rows, :], stage_im[top : top + rows, :]) for top in tops], sign
        )
        for m in range(outer):
            emit(k + inner * m, mixed[m])


def range_kernel(n_in, n_keep, tiles, widths, place_ref, *refs):
    refs = list(refs)
    u_refs = [refs.pop(0) for _ in range(n_in)]
    cr_ref, sr_ref, front_ref, back_ref, wf_ref, wi_ref = [refs.pop(0) for _ in range(6)]
    del refs[:n_keep]
    outs = [[refs.pop(0) for _ in range(tiles // 2)] for _ in widths]
    core = place_ref[0] % 2
    parts = len(refs) // 5
    rows = u_refs[0].shape[1] // parts
    count = cr_ref.shape[2] // LANES
    per_tile = count // tiles
    sizes = [u.shape[2] for u in u_refs]

    def steps_of(part):
        stage_re, stage_im, hi, lo, mid = refs[5 * part : 5 * part + 5]
        here = slice(part * rows, (part + 1) * rows)

        def load(a):
            lane, j = place(a * LANES, sizes)
            u = u_refs[j]
            return u[0, here, lane : lane + LANES], u[1, here, lane : lane + LANES]

        def put(k, re, im):
            top = k * rows
            hi[top : top + rows, :LANES], lo[top : top + rows, :LANES] = split_words(re)
            hi[top : top + rows, LANES:], lo[top : top + rows, LANES:] = split_words(im)

        def emit_front(k, value):
            re, im = value
            c, s = front_ref[0, k : k + 1, :], front_ref[1, k : k + 1, :]
            put(k, re * c - im * s, re * s + im * c)

        def front():
            sectioned_dft(load, emit_front, count, -1, stage_re, stage_im, rows)

        def mix(table_ref):
            high = hi[...]
            mid[...] = dot(jnp.concatenate([high, lo[...], high], axis=1), table_ref[...])

        def filtered():
            for k in range(count):
                top = k * rows
                re, im = mid[top : top + rows, :LANES], mid[top : top + rows, LANES:]
                c = cr_ref[0, here, k * LANES : (k + 1) * LANES]
                s = sr_ref[0, here, k * LANES : (k + 1) * LANES]
                put(k, re * c - im * s, re * s + im * c)

        def load_back(k):
            top = k * rows
            re, im = mid[top : top + rows, :LANES], mid[top : top + rows, LANES:]
            c, s = back_ref[0, k : k + 1, :], back_ref[1, k : k + 1, :]
            return re * c - im * s, re * s + im * c

        def emit_back(a, value):
            lane, j = place((a % per_tile) * LANES, widths)
            tile = a // per_tile
            out, toward = outs[j][tile // 2], (tile % 2) ^ core
            out[toward, 0, here, lane : lane + LANES] = value[0]
            out[toward, 1, here, lane : lane + LANES] = value[1]

        def back():
            sectioned_dft(load_back, emit_back, count, 1, stage_re, stage_im, rows)

        return [front, lambda: mix(wf_ref), filtered, lambda: mix(wi_ref), back]

    work = [steps_of(part) for part in range(parts)]
    for at in range(5 + 2 * parts):
        for part in range(parts):
            if 0 <= at - part < 5:
                work[part][at - part]()


def range_tables(t, tiles, count):
    k = jnp.arange(count, dtype=jnp.int32)[:, None]
    b = jnp.arange(LANES, dtype=jnp.int32)[None, :]
    extent = count * LANES
    front = jnp.stack(roots(k * b, extent, -1.0))
    back = jnp.stack(roots(k * (b + t // 2 * 2 * (extent // tiles)), extent, 1.0)) * (1.0 / extent)
    return front, back


def range_mix(sign):
    index = np.arange(LANES)
    angle = (index[:, None] * index[None, :] % LANES) * (sign * 2.0 * math.pi / LANES)
    c, s = np.cos(angle), np.sin(angle)
    table = np.block([[c, s], [-s, c]]).astype(np.float32)
    high = table.astype(jnp.bfloat16)
    low = (table - high.astype(np.float32)).astype(jnp.bfloat16)
    return jnp.asarray(np.concatenate([high, high, low], axis=0))


def range_pass(spectra, t, tiles, ranging, front, back, span, split, widths, earlier, after):
    rows = spectra[0].shape[1]
    extent = ranging[0].shape[2]
    count = extent // LANES
    block = ROW_BLOCK
    first, steps = span
    wf, wi = range_mix(-1.0), range_mix(1.0)
    in_specs = [
        pl.BlockSpec((2, block, u.shape[2]), lambda i, t: (0, first + i, 0)) for u in spectra
    ]
    in_specs += [pl.BlockSpec((1, block, extent), lambda i, t: (0, first + i, 0))] * 2
    in_specs += [pl.BlockSpec((2, count, LANES), lambda i, t: (0, 0, 0))] * 2
    in_specs += [pl.BlockSpec(wf.shape, lambda i, t: (0, 0))] * 2
    n_base = 1 + len(in_specs)
    in_specs += [ANYWHERE] * (len(earlier) + len(after))
    chips = tiles // 2
    out_specs, out_shape = [], []
    for j, out_width in enumerate(widths):
        lead = 0 if j < split else first
        out_rows = steps * block if j < split else rows
        spec = pl.BlockSpec(
            (2, 2, block, out_width), lambda i, t, lead=lead: (0, 0, lead + i, 0)
        )
        out_specs += [spec] * chips
        out_shape += [jax.ShapeDtypeStruct((2, 2, out_rows, out_width), F32)] * chips
    aliases = {n_base + i: split * chips + i for i in range(len(earlier))}
    flat = pl.pallas_call(
        functools.partial(range_kernel, len(spectra), len(earlier) + len(after), tiles, widths),
        grid_spec=pltpu.PrefetchScalarGridSpec(
            num_scalar_prefetch=1,
            grid=(steps,),
            in_specs=in_specs,
            out_specs=out_specs,
            scratch_shapes=[
                pltpu.VMEM((count * PART_ROWS, LANES), F32),
                pltpu.VMEM((count * PART_ROWS, LANES), F32),
                pltpu.VMEM((count * PART_ROWS, 2 * LANES), BF16),
                pltpu.VMEM((count * PART_ROWS, 2 * LANES), BF16),
                pltpu.VMEM((count * PART_ROWS, 2 * LANES), F32),
            ]
            * (block // PART_ROWS),
        ),
        out_shape=out_shape,
        input_output_aliases=aliases,
        compiler_params=params(),
        cost_estimate=cost(),
        name="range_filter",
    )(t, *spectra, *ranging, front, back, wf, wi, *earlier, *after)
    return [flat[j * chips : (j + 1) * chips] for j in range(len(widths))]


def azimuth_back_kernel(layout, blocks, place_ref, high_ref, low_ref, cos_ref, sin_ref, *refs):
    total = sum(len(rows) for rows in layout)
    pieces, (outs, kbuf, z) = refs[:total], (refs[-2 - len(blocks) : -2], refs[-2], refs[-1])
    grouped, at = [], 0
    for rows in layout:
        grouped.append(list(zip(rows, pieces[at : at + len(rows)])))
        at += len(rows)
    per = cos_ref.shape[1] // RADIX
    mixed_rows = z.shape[1] // 2
    tiles = len(layout)
    for a in range(RADIX):
        for r, group in enumerate(grouped):
            owner = lax.rem(place_ref[0] + tiles - r // 2 * 2, tiles) ^ (r % 2)
            first, low = 0, a * per
            for rows, piece in group:
                high = min((a + 1) * per, first + rows)
                if first <= low < high:
                    c, s = cos_ref[owner, low:high, :], sin_ref[owner, low:high, :]
                    re = piece[0, 0, low - first : high - first, :]
                    im = piece[0, 1, low - first : high - first, :]
                    top = pl.ds(pl.multiple_of(owner * per + low - a * per, 8), high - low)
                    kbuf[0, top, :] = re * c - im * s
                    kbuf[1, top, :] = re * s + im * c
                    low = high
                first += rows
        hi, lo = split_words(kbuf[...].reshape(z.shape[1:]))
        z[a] = dot(high_ref[a], hi) + dot(high_ref[a], lo) + dot(low_ref[a], hi)
    for low in range(0, mixed_rows, 8):
        values = [
            (z[a, low : low + 8, :], z[a, mixed_rows + low : mixed_rows + low + 8, :])
            for a in range(RADIX)
        ]
        for p, value in enumerate(short_dft(values, 1)):
            p, n = place(p, blocks)
            ref, top = outs[n], p * mixed_rows + low
            ref[0, top : top + 8, :] = value[0]
            ref[1, top : top + 8, :] = value[1]


def azimuth_back(pieces, t, turns, table, column, blocks, after=()):
    flat = [piece for group in pieces for piece in group]
    layout = [[piece.shape[2] for piece in group] for group in pieces]
    width = flat[0].shape[3]
    tiles, rows, _ = turns[0].shape
    double = table[0].shape[1]
    outs = [jax.ShapeDtypeStruct((2, n * double // 2, width), F32) for n in blocks]
    whole = pl.BlockSpec(table[0].shape, lambda i, t: (0, 0, 0))
    turn = pl.BlockSpec((tiles, rows, width), lambda i, t: (0, 0, column // width))
    return pl.pallas_call(
        functools.partial(azimuth_back_kernel, layout, blocks),
        grid_spec=pltpu.PrefetchScalarGridSpec(
            num_scalar_prefetch=1,
            grid=(1,),
            in_specs=[whole, whole, turn, turn]
            + [pl.BlockSpec((1, *piece.shape[1:]), lambda i, t: (0, 0, 0, 0)) for piece in flat]
            + [ANYWHERE] * len(after),
            out_specs=[pl.BlockSpec(out.shape, lambda i, t: (0, 0, 0)) for out in outs],
            scratch_shapes=[
                pltpu.VMEM((2, double // 2, width), F32),
                pltpu.VMEM((RADIX, double, width), F32),
            ],
        ),
        out_shape=outs,
        compiler_params=params(24),
        cost_estimate=cost(),
        name="azimuth_back",
    )(t, *table, *turns, *flat, *after)


def azimuth_back_table(extent):
    index = np.arange(extent // RADIX)
    doppler = RADIX * index[None, :] + np.arange(RADIX)[:, None]
    residue = doppler[:, None, :] * index[None, :, None] % extent
    angle = residue * (2.0 * math.pi / extent)
    return split_table(complex_blocks(np.cos(angle), np.sin(angle)) / extent)


def add_kernel(parts, head_ref, *refs):
    top = 0
    for part in refs[:parts]:
        rows = slice(top, top + part.shape[1])
        refs[-1][:, rows] = head_ref[:, rows] + part[...]
        top += part.shape[1]


def add_tail(head, tail, earlier, column, full_width):
    _, rows, width = head.shape
    kept = [] if earlier is None else [earlier]
    return pl.pallas_call(
        functools.partial(add_kernel, len(tail)),
        grid=(1,),
        in_specs=[
            pl.BlockSpec((2, part.shape[1], width), lambda i: (0, 0, 0)) for part in (head, *tail)
        ]
        + [ANYWHERE] * len(kept),
        out_specs=pl.BlockSpec((2, rows, width), lambda i: (0, 0, column // width)),
        out_shape=jax.ShapeDtypeStruct((2, rows, full_width), F32),
        input_output_aliases={1 + len(tail): 0} if kept else {},
        compiler_params=params(),
        cost_estimate=cost(),
        name="add_tail",
    )(head, *tail, *kept)


def scaling_cuts(phase_scaling, rows):
    tiles = lax.axis_size("tile")
    t = lax.axis_index("tile")
    copies = lax.axis_size("strip") * lax.axis_size("az")
    replica = lax.axis_index("strip") * lax.axis_size("az") + lax.axis_index("az")
    share = rows // copies

    def rows_at(start, size):
        return lax.dynamic_slice(phase_scaling, (start, 0), (size, phase_scaling.shape[1]))

    near = [rows_at((t ^ q) * rows, rows) for q in range(2)]
    far = [rows_at((t ^ q) * rows + replica * share, share) for q in range(2, tiles)]
    return near, far


def halves(piece):
    rows = piece.shape[2]
    cut = rows // 2 if rows >= 256 else rows
    return [piece[1:, :, low : low + cut] for low in range(0, rows, cut)]


def body(raw_echo, phase_scaling, phase_range, phase_azimuth):
    tiles = lax.axis_size("tile")
    t = lax.axis_index("tile")
    place_t = t.reshape(1)
    per, ranges = raw_echo.shape[1:]
    extent, width = phase_scaling.shape
    rows = phase_range.shape[0]
    count = ranges // LANES
    index = jnp.arange(tiles, dtype=jnp.int32)

    near, far = scaling_cuts(phase_scaling, rows)
    far_sent = [exchange(cut, q + 2) for q, cut in enumerate(far)]

    part = ranges // 8
    straight, at = [], 0
    for size in (4 * part, 3 * part, part):
        piece = gate(raw_echo[:, :, at : at + size], *far_sent)
        at += size
        straight.append([piece] + [exchange(piece, q) for q in range(2, tiles, 2)])

    far_all = lax.all_gather(jnp.stack(far_sent), ("strip", "az"))
    near[1] = exchange(near[1], 1)

    permuted = phase_range.reshape(rows, LANES, count).transpose(0, 2, 1).reshape(1, rows, ranges)
    ranging = turns_of(permuted, jnp.zeros((1,), jnp.int32))
    azimuth = turns_of(phase_azimuth.reshape(tiles, rows, width), index, after=[ranging[0]])
    front, back = range_tables(t, tiles, count)
    front_table = azimuth_front_table(tiles, per * tiles, rows, extent)
    back_table = azimuth_back_table(extent)

    tokens = [azimuth[0], front, back]
    far_rows = gate(far_all, *tokens).transpose(1, 0, 2, 3).reshape(tiles - 2, rows, width)
    pieces = jnp.concatenate([near[0][None], near[1][None], far_rows])
    scaling = turns_of(pieces, t ^ index, after=[azimuth[0]])
    spectra, column = [], 0
    for received in straight:
        received = [gate(piece, *tokens) for piece in received]
        handed = [exchange(piece, 1) for piece in received]
        got = [piece for pair in zip(received, handed) for piece in pair]
        spectra.append(azimuth_front(got, place_t, front_table, scaling, column))
        column += received[0].shape[2]
        tokens = [spectra[-1]]

    if width >= 8 * LANES:
        widths = [width // 4] * 4
    else:
        widths = [LANES] * (width // LANES)
    blocks = rows // ROW_BLOCK
    spans = [(0, blocks)] if blocks < 8 else [(0, blocks // 2), (blocks // 2, blocks // 2)]
    split = 1 if len(spans) > 1 else 0
    parts, kept, sequence = [], [], []
    for span in spans:
        done = range_pass(
            spectra, place_t, tiles, ranging, front, back, span, split, widths, kept, []
        )
        parts.append([to_chips(chunk, sequence, 1) for chunk in done[:split]])
        kept = [piece for chunk in done[split:] for piece in chunk]
    ready = [[part[j] for part in parts] for j in range(split)]
    for j, chunk in enumerate(done[split:]):
        ready.append([to_chips(chunk, sequence, min(j + 1, 2))])

    heads, tails, images, column = [], [], [], 0
    for j in range(len(widths)):
        tokens = heads[-1:] + (tails[j - 2] if j >= 2 else [])
        groups = [[gate(piece, *tokens) for piece in group] for group in ready[j]]
        pieces = []
        for k in range(tiles // 2):
            pieces.append([group[k] for group in groups])
            pieces.append([exchange(part, 1) for group in groups for part in halves(group[k])])
        half = RADIX // 2
        is_last = j == len(widths) - 1
        blocks = (half, half - 1, 1) if is_last else (half, half)
        head, *tail = azimuth_back(
            pieces, place_t, azimuth, back_table, column, blocks, after=heads[-1:]
        )
        heads.append(head)
        if is_last and tails:
            tail[-1] = gate(tail[-1], *tails[-1])
        tails.append([from_behind(part, "az") for part in tail])
        if j >= 1:
            image = images[-1] if images else None
            images.append(
                add_tail(heads[j - 1], tails[j - 1], image, column - widths[j - 1], width)
            )
        column += widths[j]
    image = images[-1] if images else None
    return add_tail(heads[-1], tails[-1], image, column - widths[-1], width)


def solution(mesh):
    return jax.shard_map(
        body,
        mesh=mesh,
        in_specs=(
            P(None, ("strip", "az", "tile"), None),
            P(None, "tile"),
            P("tile", None),
            P(None, "tile"),
        ),
        out_specs=P(None, ("strip", "az"), "tile"),
        check_vma=False,
    )
```

```python
import functools
import math

import jax
import jax.numpy as jnp
import numpy as np
from jax import lax
from jax.experimental import pallas as pl
from jax.experimental.pallas import tpu as pltpu
from jax.sharding import PartitionSpec as P

F32 = jnp.float32
BF16 = jnp.bfloat16
LANES = 128
ROW_BLOCK = 32
PART_ROWS = 16
RADIX = 8
MEBI = 1024 * 1024
ANYWHERE = pl.BlockSpec(memory_space=pl.ANY)


def params(mebibytes=16):
    return pltpu.CompilerParams(vmem_limit_bytes=mebibytes * MEBI)


def cost():
    return pl.CostEstimate(flops=1024, bytes_accessed=1024, transcendentals=0)


def from_behind(value, axis):
    length = lax.axis_size(axis)
    return lax.ppermute(value, axis, [(i, i + 1) for i in range(length - 1)])


def exchange(value, mask):
    length = lax.axis_size("tile")
    return lax.ppermute(value, "tile", [(i, i ^ mask) for i in range(length)])


def shift(value, by):
    length = lax.axis_size("tile")
    return lax.ppermute(value, "tile", [(i, (i + by) % length) for i in range(length)])


def to_chips(pieces, arrived, last=2):
    tokens = arrived[-last] if len(arrived) >= last else []
    got = [shift(gate(piece, *tokens), 2 * k) for k, piece in enumerate(pieces) if k > 0]
    arrived.append(got)
    return [pieces[0]] + got


def gate(value, *tokens):
    return lax.optimization_barrier((value, *tokens))[0]


def split_words(value):
    high = value.astype(BF16)
    low = (value - high.astype(F32)).astype(BF16)
    return high, low


def split_table(table):
    table = table.astype(np.float32)
    high = table.astype(jnp.bfloat16)
    return high, (table - high.astype(np.float32)).astype(jnp.bfloat16)


def complex_blocks(c, s):
    return np.concatenate(
        [np.concatenate([c, -s], axis=-1), np.concatenate([s, c], axis=-1)], axis=-2
    )


def roots(residue, modulus, sign):
    angle = (residue % modulus).astype(F32) * (sign * 2.0 * math.pi / modulus)
    return jnp.cos(angle), jnp.sin(angle)


def place(offset, sizes):
    j = 0
    while offset >= sizes[j]:
        offset -= sizes[j]
        j += 1
    return offset, j


def dot(left, right):
    return jnp.dot(left, right, preferred_element_type=F32)


def times_root(value, numerator, denominator):
    re, im = value
    eighths = 8 * (numerator % denominator)
    if eighths % denominator == 0:
        octant = eighths // denominator
        half = math.sqrt(0.5)
        if octant == 0:
            return re, im
        if octant == 1:
            return (re - im) * half, (re + im) * half
        if octant == 2:
            return -im, re
        if octant == 3:
            return (re + im) * -half, (re - im) * half
        if octant == 4:
            return -re, -im
        if octant == 5:
            return (im - re) * half, (re + im) * -half
        if octant == 6:
            return im, -re
        return (re + im) * half, (im - re) * half
    angle = 2.0 * math.pi * (numerator % denominator) / denominator
    c, s = math.cos(angle), math.sin(angle)
    return re * c - im * s, re * s + im * c


def short_dft(values, sign):
    count = len(values)
    if count == 1:
        return values
    even = short_dft(values[0::2], sign)
    odd = short_dft(values[1::2], sign)
    low, high = [], []
    for k in range(count // 2):
        re, im = times_root(odd[k], sign * k, count)
        low.append((even[k][0] + re, even[k][1] + im))
        high.append((even[k][0] - re, even[k][1] - im))
    return low + high


def cos_sin(angle):
    turns = jnp.round(angle * (2.0 / math.pi))
    rest = (angle - turns * 1.57079637050628662109375) - turns * -4.37113900018624283e-8
    sq = rest * rest
    sin_r = rest + rest * sq * (-1.6666654611e-1 + sq * (8.3321608736e-3 + sq * -1.9515295891e-4))
    cos_r = 1.0 - 0.5 * sq + sq * sq * (
        4.166664568298827e-2 + sq * (-1.388731625493765e-3 + sq * 2.443315711809948e-5)
    )
    size = jnp.abs(turns)
    odd = size == 1.0
    flip = 1.0 - size
    return (
        jnp.where(odd, -turns * sin_r, flip * cos_r),
        jnp.where(odd, turns * cos_r, flip * sin_r),
    )


def turn_kernel(order_ref, phase_ref, *refs):
    cos_ref, sin_ref, column = refs[-3:]
    per = phase_ref.shape[1] // RADIX
    for lane in range(0, phase_ref.shape[2], LANES):
        column[...] = phase_ref[0, :, lane : lane + LANES]
        for a in range(RADIX):
            c, s = cos_sin(column[pl.ds(a, per, stride=RADIX), :])
            cos_ref[0, a * per : (a + 1) * per, lane : lane + LANES] = c
            sin_ref[0, a * per : (a + 1) * per, lane : lane + LANES] = s


def turns_of(phase, order, after=()):
    blocks, rows, width = phase.shape
    step = min(width, 512)
    shape = jax.ShapeDtypeStruct(phase.shape, F32)
    spec = pl.BlockSpec((1, rows, step), lambda i, j, order: (i, 0, j))
    return pl.pallas_call(
        turn_kernel,
        grid_spec=pltpu.PrefetchScalarGridSpec(
            num_scalar_prefetch=1,
            grid=(blocks, width // step),
            in_specs=[pl.BlockSpec((1, rows, step), lambda i, j, order: (order[i], 0, j))]
            + [ANYWHERE] * len(after),
            out_specs=[spec, spec],
            scratch_shapes=[pltpu.VMEM((rows, LANES), F32)],
        ),
        out_shape=[shape, shape],
        compiler_params=params(),
        cost_estimate=cost(),
        name="phase_turns",
    )(order, phase, *after)


def azimuth_front_kernel(count, place_ref, high_ref, low_ref, cos_ref, sin_ref, *refs):
    pieces, (out_ref, hi, lo) = refs[:count], refs[-3:]
    per = pieces[0].shape[1]
    half = hi.shape[0] // 2
    rows = out_ref.shape[1]
    for q in range(count):
        owner = place_ref[0] ^ q
        for part in range(2):
            top = pl.ds(pl.multiple_of(part * half + owner * per, per), per)
            hi[top, :], lo[top, :] = split_words(pieces[q][part])
    mixed = dot(high_ref[0], hi[...]) + dot(high_ref[0], lo[...]) + dot(low_ref[0], hi[...])
    re, im = mixed[:rows], mixed[rows:]
    c, s = cos_ref[0], sin_ref[0]
    out_ref[0] = re * c - im * s
    out_ref[1] = re * s + im * c


def azimuth_front(pieces, t, table, scaling, column):
    count = len(pieces)
    per, width = pieces[0].shape[1:]
    _, double, depth = table[0].shape
    step = min(256, scaling[0].shape[2])
    per_tile = scaling[0].shape[2] // step
    first = column // step
    whole = pl.BlockSpec((1, double, depth), lambda i, t: (t[0], 0, 0))
    turn = pl.BlockSpec(
        (1, double // 2, step), lambda i, t: ((first + i) // per_tile, 0, (first + i) % per_tile)
    )
    return pl.pallas_call(
        functools.partial(azimuth_front_kernel, count),
        grid_spec=pltpu.PrefetchScalarGridSpec(
            num_scalar_prefetch=1,
            grid=(width // step,),
            in_specs=[whole, whole, turn, turn]
            + [pl.BlockSpec((2, per, step), lambda i, t: (0, 0, i))] * count,
            out_specs=pl.BlockSpec((2, double // 2, step), lambda i, t: (0, 0, i)),
            scratch_shapes=[pltpu.VMEM((depth, step), BF16)] * 2,
        ),
        out_shape=jax.ShapeDtypeStruct((2, double // 2, width), F32),
        compiler_params=params(),
        cost_estimate=cost(),
        name="azimuth_front",
    )(t, *table, *scaling, *pieces)


def azimuth_front_table(tiles, pulses, rows, extent):
    local = np.arange(rows).reshape(rows // RADIX, RADIX).T.reshape(-1)
    doppler = np.arange(tiles)[:, None] * rows + local[None, :]
    residue = doppler[:, :, None] * np.arange(pulses) % extent
    angle = residue * (-2.0 * math.pi / extent)
    return split_table(complex_blocks(np.cos(angle), np.sin(angle)))


def sectioned_dft(load, emit, count, sign, stage_re, stage_im, rows):
    inner = min(8, count)
    outer = count // inner
    for a0 in range(outer):
        mixed = short_dft([load(outer * a1 + a0) for a1 in range(inner)], sign)
        for k in range(inner):
            re, im = times_root(mixed[k], sign * a0 * k, count)
            top = (a0 * inner + k) * rows
            stage_re[top : top + rows, :] = re
            stage_im[top : top + rows, :] = im
    for k in range(inner):
        tops = [(a0 * inner + k) * rows for a0 in range(outer)]
        mixed = short_dft(
            [(stage_re[top : top + rows, :], stage_im[top : top + rows, :]) for top in tops], sign
        )
        for m in range(outer):
            emit(k + inner * m, mixed[m])


def range_kernel(n_in, n_keep, tiles, widths, place_ref, *refs):
    refs = list(refs)
    u_refs = [refs.pop(0) for _ in range(n_in)]
    cr_ref, sr_ref, front_ref, back_ref, wf_ref, wi_ref = [refs.pop(0) for _ in range(6)]
    del refs[:n_keep]
    outs = [[refs.pop(0) for _ in range(tiles // 2)] for _ in widths]
    core = place_ref[0] % 2
    parts = len(refs) // 5
    rows = u_refs[0].shape[1] // parts
    count = cr_ref.shape[2] // LANES
    per_tile = count // tiles
    sizes = [u.shape[2] for u in u_refs]

    def steps_of(part):
        stage_re, stage_im, hi, lo, mid = refs[5 * part : 5 * part + 5]
        here = slice(part * rows, (part + 1) * rows)

        def load(a):
            lane, j = place(a * LANES, sizes)
            u = u_refs[j]
            return u[0, here, lane : lane + LANES], u[1, here, lane : lane + LANES]

        def put(k, re, im):
            top = k * rows
            hi[top : top + rows, :LANES], lo[top : top + rows, :LANES] = split_words(re)
            hi[top : top + rows, LANES:], lo[top : top + rows, LANES:] = split_words(im)

        def emit_front(k, value):
            re, im = value
            c, s = front_ref[0, k : k + 1, :], front_ref[1, k : k + 1, :]
            put(k, re * c - im * s, re * s + im * c)

        def front():
            sectioned_dft(load, emit_front, count, -1, stage_re, stage_im, rows)

        def mix(table_ref):
            high = hi[...]
            mid[...] = dot(jnp.concatenate([high, lo[...], high], axis=1), table_ref[...])

        def filtered():
            for k in range(count):
                top = k * rows
                re, im = mid[top : top + rows, :LANES], mid[top : top + rows, LANES:]
                c = cr_ref[0, here, k * LANES : (k + 1) * LANES]
                s = sr_ref[0, here, k * LANES : (k + 1) * LANES]
                put(k, re * c - im * s, re * s + im * c)

        def load_back(k):
            top = k * rows
            re, im = mid[top : top + rows, :LANES], mid[top : top + rows, LANES:]
            c, s = back_ref[0, k : k + 1, :], back_ref[1, k : k + 1, :]
            return re * c - im * s, re * s + im * c

        def emit_back(a, value):
            lane, j = place((a % per_tile) * LANES, widths)
            tile = a // per_tile
            out, toward = outs[j][tile // 2], (tile % 2) ^ core
            out[toward, 0, here, lane : lane + LANES] = value[0]
            out[toward, 1, here, lane : lane + LANES] = value[1]

        def back():
            sectioned_dft(load_back, emit_back, count, 1, stage_re, stage_im, rows)

        return [front, lambda: mix(wf_ref), filtered, lambda: mix(wi_ref), back]

    work = [steps_of(part) for part in range(parts)]
    for at in range(5 + 2 * parts):
        for part in range(parts):
            if 0 <= at - part < 5:
                work[part][at - part]()


def range_tables(t, tiles, count):
    k = jnp.arange(count, dtype=jnp.int32)[:, None]
    b = jnp.arange(LANES, dtype=jnp.int32)[None, :]
    extent = count * LANES
    front = jnp.stack(roots(k * b, extent, -1.0))
    back = jnp.stack(roots(k * (b + t // 2 * 2 * (extent // tiles)), extent, 1.0)) * (1.0 / extent)
    return front, back


def range_mix(sign):
    index = np.arange(LANES)
    angle = (index[:, None] * index[None, :] % LANES) * (sign * 2.0 * math.pi / LANES)
    c, s = np.cos(angle), np.sin(angle)
    table = np.block([[c, s], [-s, c]]).astype(np.float32)
    high = table.astype(jnp.bfloat16)
    low = (table - high.astype(np.float32)).astype(jnp.bfloat16)
    return jnp.asarray(np.concatenate([high, high, low], axis=0))


def range_pass(spectra, t, tiles, ranging, front, back, span, split, widths, earlier, after):
    rows = spectra[0].shape[1]
    extent = ranging[0].shape[2]
    count = extent // LANES
    block = ROW_BLOCK
    first, steps = span
    wf, wi = range_mix(-1.0), range_mix(1.0)
    in_specs = [
        pl.BlockSpec((2, block, u.shape[2]), lambda i, t: (0, first + i, 0)) for u in spectra
    ]
    in_specs += [pl.BlockSpec((1, block, extent), lambda i, t: (0, first + i, 0))] * 2
    in_specs += [pl.BlockSpec((2, count, LANES), lambda i, t: (0, 0, 0))] * 2
    in_specs += [pl.BlockSpec(wf.shape, lambda i, t: (0, 0))] * 2
    n_base = 1 + len(in_specs)
    in_specs += [ANYWHERE] * (len(earlier) + len(after))
    chips = tiles // 2
    out_specs, out_shape = [], []
    for j, out_width in enumerate(widths):
        lead = 0 if j < split else first
        out_rows = steps * block if j < split else rows
        spec = pl.BlockSpec(
            (2, 2, block, out_width), lambda i, t, lead=lead: (0, 0, lead + i, 0)
        )
        out_specs += [spec] * chips
        out_shape += [jax.ShapeDtypeStruct((2, 2, out_rows, out_width), F32)] * chips
    aliases = {n_base + i: split * chips + i for i in range(len(earlier))}
    flat = pl.pallas_call(
        functools.partial(range_kernel, len(spectra), len(earlier) + len(after), tiles, widths),
        grid_spec=pltpu.PrefetchScalarGridSpec(
            num_scalar_prefetch=1,
            grid=(steps,),
            in_specs=in_specs,
            out_specs=out_specs,
            scratch_shapes=[
                pltpu.VMEM((count * PART_ROWS, LANES), F32),
                pltpu.VMEM((count * PART_ROWS, LANES), F32),
                pltpu.VMEM((count * PART_ROWS, 2 * LANES), BF16),
                pltpu.VMEM((count * PART_ROWS, 2 * LANES), BF16),
                pltpu.VMEM((count * PART_ROWS, 2 * LANES), F32),
            ]
            * (block // PART_ROWS),
        ),
        out_shape=out_shape,
        input_output_aliases=aliases,
        compiler_params=params(),
        cost_estimate=cost(),
        name="range_filter",
    )(t, *spectra, *ranging, front, back, wf, wi, *earlier, *after)
    return [flat[j * chips : (j + 1) * chips] for j in range(len(widths))]


def azimuth_back_kernel(layout, blocks, place_ref, high_ref, low_ref, cos_ref, sin_ref, *refs):
    total = sum(len(rows) for rows in layout)
    pieces, (outs, kbuf, z) = refs[:total], (refs[-2 - len(blocks) : -2], refs[-2], refs[-1])
    grouped, at = [], 0
    for rows in layout:
        grouped.append(list(zip(rows, pieces[at : at + len(rows)])))
        at += len(rows)
    per = cos_ref.shape[1] // RADIX
    mixed_rows = z.shape[1] // 2
    tiles = len(layout)
    for a in range(RADIX):
        for r, group in enumerate(grouped):
            owner = lax.rem(place_ref[0] + tiles - r // 2 * 2, tiles) ^ (r % 2)
            first, low = 0, a * per
            for rows, piece in group:
                high = min((a + 1) * per, first + rows)
                if first <= low < high:
                    c, s = cos_ref[owner, low:high, :], sin_ref[owner, low:high, :]
                    re = piece[0, 0, low - first : high - first, :]
                    im = piece[0, 1, low - first : high - first, :]
                    top = pl.ds(pl.multiple_of(owner * per + low - a * per, 8), high - low)
                    kbuf[0, top, :] = re * c - im * s
                    kbuf[1, top, :] = re * s + im * c
                    low = high
                first += rows
        hi, lo = split_words(kbuf[...].reshape(z.shape[1:]))
        z[a] = dot(high_ref[a], hi) + dot(high_ref[a], lo) + dot(low_ref[a], hi)
    for low in range(0, mixed_rows, 8):
        values = [
            (z[a, low : low + 8, :], z[a, mixed_rows + low : mixed_rows + low + 8, :])
            for a in range(RADIX)
        ]
        for p, value in enumerate(short_dft(values, 1)):
            p, n = place(p, blocks)
            ref, top = outs[n], p * mixed_rows + low
            ref[0, top : top + 8, :] = value[0]
            ref[1, top : top + 8, :] = value[1]


def azimuth_back(pieces, t, turns, table, column, blocks, after=()):
    flat = [piece for group in pieces for piece in group]
    layout = [[piece.shape[2] for piece in group] for group in pieces]
    width = flat[0].shape[3]
    tiles, rows, _ = turns[0].shape
    double = table[0].shape[1]
    outs = [jax.ShapeDtypeStruct((2, n * double // 2, width), F32) for n in blocks]
    whole = pl.BlockSpec(table[0].shape, lambda i, t: (0, 0, 0))
    turn = pl.BlockSpec((tiles, rows, width), lambda i, t: (0, 0, column // width))
    return pl.pallas_call(
        functools.partial(azimuth_back_kernel, layout, blocks),
        grid_spec=pltpu.PrefetchScalarGridSpec(
            num_scalar_prefetch=1,
            grid=(1,),
            in_specs=[whole, whole, turn, turn]
            + [pl.BlockSpec((1, *piece.shape[1:]), lambda i, t: (0, 0, 0, 0)) for piece in flat]
            + [ANYWHERE] * len(after),
            out_specs=[pl.BlockSpec(out.shape, lambda i, t: (0, 0, 0)) for out in outs],
            scratch_shapes=[
                pltpu.VMEM((2, double // 2, width), F32),
                pltpu.VMEM((RADIX, double, width), F32),
            ],
        ),
        out_shape=outs,
        compiler_params=params(24),
        cost_estimate=cost(),
        name="azimuth_back",
    )(t, *table, *turns, *flat, *after)


def azimuth_back_table(extent):
    index = np.arange(extent // RADIX)
    doppler = RADIX * index[None, :] + np.arange(RADIX)[:, None]
    residue = doppler[:, None, :] * index[None, :, None] % extent
    angle = residue * (2.0 * math.pi / extent)
    return split_table(complex_blocks(np.cos(angle), np.sin(angle)) / extent)


def add_kernel(parts, head_ref, *refs):
    top = 0
    for part in refs[:parts]:
        rows = slice(top, top + part.shape[1])
        refs[-1][:, rows] = head_ref[:, rows] + part[...]
        top += part.shape[1]


def add_tail(head, tail, earlier, column, full_width):
    _, rows, width = head.shape
    kept = [] if earlier is None else [earlier]
    return pl.pallas_call(
        functools.partial(add_kernel, len(tail)),
        grid=(1,),
        in_specs=[
            pl.BlockSpec((2, part.shape[1], width), lambda i: (0, 0, 0)) for part in (head, *tail)
        ]
        + [ANYWHERE] * len(kept),
        out_specs=pl.BlockSpec((2, rows, width), lambda i: (0, 0, column // width)),
        out_shape=jax.ShapeDtypeStruct((2, rows, full_width), F32),
        input_output_aliases={1 + len(tail): 0} if kept else {},
        compiler_params=params(),
        cost_estimate=cost(),
        name="add_tail",
    )(head, *tail, *kept)


def scaling_cuts(phase_scaling, rows):
    tiles = lax.axis_size("tile")
    t = lax.axis_index("tile")
    copies = lax.axis_size("strip") * lax.axis_size("az")
    replica = lax.axis_index("strip") * lax.axis_size("az") + lax.axis_index("az")
    share = rows // copies

    def rows_at(start, size):
        return lax.dynamic_slice(phase_scaling, (start, 0), (size, phase_scaling.shape[1]))

    near = [rows_at((t ^ q) * rows, rows) for q in range(2)]
    far = [rows_at((t ^ q) * rows + replica * share, share) for q in range(2, tiles)]
    return near, far


def halves(piece):
    rows = piece.shape[2]
    cut = rows // 2 if rows >= 256 else rows
    return [piece[1:, :, low : low + cut] for low in range(0, rows, cut)]


def body(raw_echo, phase_scaling, phase_range, phase_azimuth):
    tiles = lax.axis_size("tile")
    t = lax.axis_index("tile")
    place_t = t.reshape(1)
    per, ranges = raw_echo.shape[1:]
    extent, width = phase_scaling.shape
    rows = phase_range.shape[0]
    count = ranges // LANES
    index = jnp.arange(tiles, dtype=jnp.int32)

    near, far = scaling_cuts(phase_scaling, rows)
    far_sent = [exchange(cut, q + 2) for q, cut in enumerate(far)]

    part = ranges // 8
    straight, at = [], 0
    for size in (4 * part, 3 * part, part):
        piece = gate(raw_echo[:, :, at : at + size], *far_sent)
        at += size
        straight.append([piece] + [exchange(piece, q) for q in range(2, tiles, 2)])

    far_all = lax.all_gather(jnp.stack(far_sent), ("strip", "az"))
    near[1] = exchange(near[1], 1)

    permuted = phase_range.reshape(rows, LANES, count).transpose(0, 2, 1).reshape(1, rows, ranges)
    ranging = turns_of(permuted, jnp.zeros((1,), jnp.int32))
    azimuth = turns_of(phase_azimuth.reshape(tiles, rows, width), index, after=[ranging[0]])
    front, back = range_tables(t, tiles, count)
    front_table = azimuth_front_table(tiles, per * tiles, rows, extent)
    back_table = azimuth_back_table(extent)

    tokens = [azimuth[0], front, back]
    far_rows = gate(far_all, *tokens).transpose(1, 0, 2, 3).reshape(tiles - 2, rows, width)
    pieces = jnp.concatenate([near[0][None], near[1][None], far_rows])
    scaling = turns_of(pieces, t ^ index, after=[azimuth[0]])
    spectra, column = [], 0
    for received in straight:
        received = [gate(piece, *tokens) for piece in received]
        handed = [exchange(piece, 1) for piece in received]
        got = [piece for pair in zip(received, handed) for piece in pair]
        spectra.append(azimuth_front(got, place_t, front_table, scaling, column))
        column += received[0].shape[2]
        tokens = [spectra[-1]]

    if width >= 8 * LANES:
        widths = [width // 4] * 4
    else:
        widths = [LANES] * (width // LANES)
    blocks = rows // ROW_BLOCK
    spans = [(0, blocks)] if blocks < 8 else [(0, blocks // 2), (blocks // 2, blocks // 2)]
    split = 1 if len(spans) > 1 else 0
    parts, kept, sequence = [], [], []
    for span in spans:
        done = range_pass(
            spectra, place_t, tiles, ranging, front, back, span, split, widths, kept, []
        )
        parts.append([to_chips(chunk, sequence, 1) for chunk in done[:split]])
        kept = [piece for chunk in done[split:] for piece in chunk]
    ready = [[part[j] for part in parts] for j in range(split)]
    for j, chunk in enumerate(done[split:]):
        ready.append([to_chips(chunk, sequence, min(j + 1, 2))])

    heads, tails, images, column = [], [], [], 0
    for j in range(len(widths)):
        tokens = heads[-1:] + (tails[j - 2] if j >= 2 else [])
        groups = [
            [gate(piece, *(tokens if k else heads[-1:])) for k, piece in enumerate(group)]
            for group in ready[j]
        ]
        pieces = []
        for k in range(tiles // 2):
            pieces.append([group[k] for group in groups])
            pieces.append([exchange(part, 1) for group in groups for part in halves(group[k])])
        half = RADIX // 2
        is_last = j == len(widths) - 1
        blocks = (half, half - 1, 1) if is_last else (half, half)
        head, *tail = azimuth_back(
            pieces, place_t, azimuth, back_table, column, blocks, after=heads[-1:]
        )
        heads.append(head)
        if is_last and tails:
            tail[-1] = gate(tail[-1], *tails[-1])
        tails.append([from_behind(part, "az") for part in tail])
        if j >= 1:
            image = images[-1] if images else None
            images.append(
                add_tail(heads[j - 1], tails[j - 1], image, column - widths[j - 1], width)
            )
        column += widths[j]
    image = images[-1] if images else None
    return add_tail(heads[-1], tails[-1], image, column - widths[-1], width)


def solution(mesh):
    return jax.shard_map(
        body,
        mesh=mesh,
        in_specs=(
            P(None, ("strip", "az", "tile"), None),
            P(None, "tile"),
            P("tile", None),
            P(None, "tile"),
        ),
        out_specs=P(None, ("strip", "az"), "tile"),
        check_vma=False,
    )
```
